128 devices in a mesh: row: 8 (over y, core), col: 16 (over x, z).
Axes of the slice: x: 4, y: 4, z: 4, core: 2. Of those that a mesh axis runs over, the one named last changes fastest.
Arguments:
- kernels: bfloat16 [6, 16384, 12288], P(None, 'col', 'row'), may hold values from -0.0234375 to 0.0234375
- history: bfloat16 [6, 12288, 256], P(None, ('row', 'col')), may hold values from -6 to 6
- incident: float32 [128, 128, 256], P(('row', 'col')), may hold values from -6 to 6
- owner: int32 [128], replicated, may hold values from 0 to 7, as said below
- tile_pairs: int32 [1536, 2], P(('row', 'col')), may hold values from 0 to 127, as said below
- tile_values: bfloat16 [1536, 128, 128], P(('row', 'col')), may hold values from -0.109375 to 0.109375
- tile_counts: int32 [128], P(('row', 'col')), may hold values from 1 to 12, as said below
Outputs:
- density: float32 [128, 128, 256], P(('row', 'col'))
The draws below stay inside these ranges and needn't reach their ends.
Inputs may be any that keep to these rules, and one draw needn't show every extreme that they name: `owner`: within each block of 8 consecutive clusters starting at a multiple of 8, the owners are all different. tile_pairs[t, 0] is the cluster whose slot is t // 12; for a target cluster k the sources of its slot are distinct clusters whose block (cluster // 8) is k // 8 - 1, k // 8 or k // 8 + 1, modulo 16. `tile_counts`: some device has all 12 slots live.
All inputs are finite; a program needn't handle non-finite values.
Results may differ from the reference program's by a relative error of at most 0.0012.
Values may be sent and summed in bfloat16 or wider, within the bound.
A program may use at most 128 MiB of HBM per device.

```python
import jax
import jax.numpy as jnp
from jax import lax

LAGS = 6
CLUSTER = 128
COLUMNS = 256
TILE_DEV = 12
SWEEPS = 3
CLUSTERS = 128
TARGETS = 16384
SOURCES = 12288
N_ROW = 8
N_COL = 16


def owner_table(key):
    keys = jax.random.split(jax.random.fold_in(key, 11), N_COL)
    table = jax.vmap(lambda sub_key: jax.random.permutation(sub_key, N_ROW))(keys)
    return table.reshape(-1).astype(jnp.int32)


def draw_owner(key, part):
    return owner_table(key)


def draw_tile_pairs(key, part):
    owners = owner_table(key)
    clusters = jnp.arange(CLUSTERS, dtype=jnp.int32)
    slot_of = (owners * N_COL + clusters // N_ROW).astype(jnp.int32)
    cluster_of_slot = jnp.zeros((CLUSTERS,), jnp.int32).at[slot_of].set(clusters)
    keys = jax.random.split(jax.random.fold_in(key, 23), CLUSTERS)
    orders = jax.vmap(lambda sub_key: jax.random.permutation(sub_key, 3 * N_ROW))(keys)
    orders = orders[:, :TILE_DEV].astype(jnp.int32)
    blocks = cluster_of_slot // N_ROW
    first = (blocks + N_COL - 1) % N_COL * N_ROW
    chosen = (first[:, None] + orders) % CLUSTERS
    targets = jnp.repeat(cluster_of_slot, TILE_DEV)
    sources = chosen.reshape(-1)
    return jnp.stack([targets, sources], axis=1).astype(jnp.int32)


def draw_tile_counts(key, part):
    shifts = jax.random.randint(jax.random.fold_in(key, 31), (CLUSTERS,), 0, 4).astype(jnp.int32)
    counts = jnp.maximum(jnp.right_shift(jnp.full((CLUSTERS,), TILE_DEV, jnp.int32), shifts), 1)
    busiest = jax.random.randint(jax.random.fold_in(key, 37), (), 0, CLUSTERS)
    return counts.at[busiest].set(TILE_DEV).astype(jnp.int32)


def block_levels(rng, dims, pieces, smallest, largest):
    def one(dim, parts):
        draws = jax.random.uniform(jax.random.fold_in(jax.random.fold_in(rng, 6), dim), (parts,), jnp.float32, smallest / len(pieces), largest / len(pieces))
        return jnp.repeat(jnp.exp(draws), dims[dim] // parts).reshape((-1,) + (1,) * (len(dims) - dim - 1))

    factor_of = one(*pieces[0])
    for cut in pieces[1:]:
        factor_of = factor_of * one(*cut)
    return factor_of


def noise(own_key, shape, spread, bound, cuts=(), kind=jnp.bfloat16):
    entries = jax.random.normal(own_key, shape, jnp.float32) * spread
    if len(cuts) > 0:
        entries = block_levels(own_key, shape, cuts, -0.22, 0.18) * entries
    return jnp.clip(entries, min=-bound, max=bound).astype(kind)


def setup_inputs(seed: int = 0) -> dict:
    seeds = jax.random.split(jax.random.key(seed), 8)
    kernels = noise(seeds[0], (LAGS, TARGETS, SOURCES), (LAGS * SOURCES) ** -0.5, 0.0234375, ((1, 16), (2, 8)))
    history = noise(seeds[1], (LAGS, SOURCES, COLUMNS), 1.0, 6.0, ((1, 128),))
    incident = noise(seeds[2], (CLUSTERS, CLUSTER, COLUMNS), 1.0, 6.0, ((0, 128),), jnp.float32)
    owner = draw_owner(jax.random.fold_in(seeds[7], 71), 0)
    tile_pairs = draw_tile_pairs(jax.random.fold_in(seeds[7], 71), 0)
    tile_values = noise(seeds[5], (CLUSTERS * TILE_DEV, CLUSTER, CLUSTER), (2 * CLUSTER * TILE_DEV) ** -0.5, 0.109375, ((0, 128),))
    tile_counts = draw_tile_counts(jax.random.fold_in(seeds[7], 71), 0)
    return {"kernels": kernels, "history": history, "incident": incident, "owner": owner, "tile_pairs": tile_pairs, "tile_values": tile_values, "tile_counts": tile_counts}


damping = 0.7


def reference(kernels, history, incident, owner, tile_pairs, tile_values, tile_counts):
    retarded = jnp.zeros((TARGETS, COLUMNS), jnp.float32)
    for lag_step in range(LAGS):
        retarded = retarded + jnp.dot(kernels[lag_step], history[lag_step], preferred_element_type=jnp.float32)
    clusters = jnp.arange(CLUSTERS, dtype=jnp.int32)
    slot_of = (owner * N_COL + clusters // N_ROW).astype(jnp.int32)
    by_cluster = retarded.reshape(CLUSTERS, CLUSTER, COLUMNS)
    by_slot = jnp.zeros_like(by_cluster).at[slot_of].set(by_cluster)
    driven = incident - by_slot
    targets = tile_pairs[:, 0]
    sources = tile_pairs[:, 1]
    tgt_slot = (owner[targets] * N_COL + targets // N_ROW).astype(jnp.int32)
    src_slot = (owner[sources] * N_COL + sources // N_ROW).astype(jnp.int32)
    tile_index = jnp.arange(CLUSTERS * TILE_DEV, dtype=jnp.int32)
    holder = tile_index // TILE_DEV
    active = (tile_index % TILE_DEV < tile_counts[holder]) & (tgt_slot == holder)
    tiles_all = tile_values.reshape(CLUSTERS, TILE_DEV, CLUSTER, CLUSTER)
    slots_all = src_slot.reshape(CLUSTERS, TILE_DEV)
    flags_all = active.reshape(CLUSTERS, TILE_DEV)
    density = driven
    for sweep_step in range(SWEEPS):
        rounded = density.astype(jnp.bfloat16)

        def one_slot(inputs):
            tiles, slots, flags = inputs
            picked = jnp.where(flags[:, None, None], rounded[slots], jnp.zeros((), jnp.bfloat16))
            return lax.dot_general(tiles.astype(jnp.float32), picked.astype(jnp.float32), (((0, 2), (0, 1)), ((), ())))

        near_term = lax.map(one_slot, (tiles_all, slots_all, flags_all))
        density = density + damping * (driven - density - near_term)
    return density
```

```python
import functools

import jax
import jax.numpy as jnp
from jax import lax
from jax.experimental import pallas as pl
from jax.experimental.pallas import tpu as pltpu
from jax.sharding import PartitionSpec as P

MESH = pl.DeviceIdType.MESH
F32, BF16 = jnp.float32, jnp.bfloat16

SWEEPS = 3
DAMPING = 0.7

NX, NZ, NY = 4, 4, 4
LAGS, SRC, COLS, CL = 6, 96, 256, 128
HALVES = 2
W = COLS // HALVES
LH = LAGS // 2
DEPTH = LH * NZ * SRC
TILES = 12
TM = 512


def body(kernels, history, incident, owner, pairs, tiles, counts, out,
         hb, kb, acc, sp, rp, ts, rf, ry, inc, drv, den, tl, tcat, gat00, gat01, gat02, gat10, gat11, gat12, owner_s, pairs_s, counts_s,
         lsem, ksem, hsem, gsem, gsend, psem, psend, ysem, ysend, ssem, ssend, osem):
    row, col = lax.axis_index("row"), lax.axis_index("col")
    y, core = lax.div(row, 2), lax.rem(row, 2)
    x, z = lax.div(col, NZ), lax.rem(col, NZ)
    other = 1 - core

    def at_col(dx, dz):
        return lax.rem(x + dx + NX, NX) * NZ + lax.rem(z + dz + NZ, NZ)

    def at_row(dy):
        return lax.rem(y + dy + NY, NY) * 2 + core

    def near_col(dc):
        return lax.rem(col + dc + NX * NZ, NX * NZ)

    def send(src, dst, ssem_, rsem_, r, c):
        pltpu.make_async_remote_copy(
            src_ref=src, dst_ref=dst, send_sem=ssem_, recv_sem=rsem_,
            device_id={"row": r, "col": c}, device_id_type=MESH,
        ).start()

    def wait(ref, sem):
        pltpu.make_async_copy(ref, ref, sem).wait()

    gat = ((gat00, gat01, gat02), (gat10, gat11, gat12))

    barrier = pltpu.get_barrier_semaphore()
    greet = [(row, at_col(1, 0)), (row, at_col(-1, 0)), (row, at_col(0, 1)), (row, at_col(0, -1))]
    greet += [(at_row(dy), near_col(dc)) for dy in (-1, 0, 1) for dc in (-1, 0, 1) if dy or dc]
    greet += [(y * 2 + other, col)]
    for r, c in greet:
        pl.semaphore_signal(barrier, inc=1, device_id={"row": r, "col": c}, device_id_type=MESH)

    def piece(h, a, dx, dz, lo=0, n=SRC):
        zr = pl.multiple_of(lax.rem(z + dz + NZ, NZ) * SRC + lo, 16)
        return hb.at[h, a, dx % NX, :, pl.ds(zr, n), :]

    def own(h, a):
        return history.at[pl.ds(a * LH, LH), :, pl.ds(h * W, W)]

    for h in range(HALVES):
        for a in range(2):
            pltpu.make_async_copy(own(h, a), piece(h, a, 0, 0), hsem.at[h, a]).start()
    pltpu.make_async_copy(owner, owner_s, lsem.at[0]).start()
    pltpu.make_async_copy(pairs, pairs_s, lsem.at[1]).start()
    pltpu.make_async_copy(counts, counts_s, lsem.at[2]).start()
    pl.semaphore_wait(barrier, len(greet))

    events = []

    def at(t):
        def add(f):
            events.append((t, len(events), f))
        return add

    def axis(a, phase):
        return ((1, 0), (0, 1))[(a + phase) % 2]

    def move(h, a, off, d, lo, n, sem, first=False):
        src = own(h, a) if first else piece(h, a, off[0], off[1], lo, n)
        zr = pl.multiple_of(lax.rem(z + off[1] + NZ, NZ) * SRC + lo, 16)
        dst = hb.at[h, a, (off[0] - d[0]) % NX, :, pl.ds(zr, n), :]
        send(src, dst, gsend.at[h, 0 if d[0] else 1], sem, row, at_col(d[0], d[1]))

    def neg(d):
        return (-d[0], -d[1])

    def mul(d, k):
        return (d[0] * k, d[1] * k)

    def add2(p, q):
        return (p[0] + q[0], p[1] + q[1])

    half = SRC // 2

    def spread(h, a, off, j, first=False):
        d = axis(a, 1)
        move(h, a, off, d, 0, SRC, gsem.at[h, a, j, 0], first)
        move(h, a, off, neg(d), 0, SRC, gsem.at[h, a, j, 1], first)

    def relay(h, a, off, j, d):
        lo, hi = add2(off, neg(d)), add2(off, d)
        wait(piece(h, a, *lo), gsem.at[h, a, j, 0])
        move(h, a, lo, d, 0, half, gsem.at[h, a, j, 2])
        wait(piece(h, a, *hi), gsem.at[h, a, j, 1])
        move(h, a, hi, neg(d), half, half, gsem.at[h, a, j, 3])

    def far(h, a, off, j, d):
        o = add2(off, mul(d, 2))
        wait(piece(h, a, o[0], o[1], 0, half), gsem.at[h, a, j, 2])
        wait(piece(h, a, o[0], o[1], half, half), gsem.at[h, a, j, 3])

    started = [False] * HALVES
    kwaited = set()

    def mm(h, a, dx):
        g = a * NX + dx % NX
        if g not in kwaited:
            kwaited.add(g)
            for l in range(LH):
                wait(kb.at[g, :, pl.ds(l * NZ * SRC, NZ * SRC)], ksem.at[g, l])
        first = not started[h]
        started[h] = True

        def step(i, carry):
            rows = pl.ds(pl.multiple_of(i * TM, TM), TM)
            blocks = pl.ds(i * (TM // CL), TM // CL)
            d = jnp.dot(kb[g, rows, :], hb[h, a, dx % NX].reshape(DEPTH, W), preferred_element_type=F32)
            d = d.reshape(TM // CL, CL, W)
            acc[h, blocks] = d if first else acc[h, blocks] + d
            return carry

        lax.fori_loop(0, NX * NZ // 2 * CL // TM, step, 0)

    def gather(h, t0, u):
        @at(t0)
        def _():
            for a in range(2):
                d = axis(a, 0)
                move(h, a, (0, 0), d, 0, SRC, gsem.at[h, a, 0, 0], True)
                move(h, a, (0, 0), neg(d), 0, SRC, gsem.at[h, a, 0, 1], True)
            for a in range(2):
                spread(h, a, (0, 0), 1, True)
            if h == 0:
                order = [(1, 0), (0, 0), (1, 3), (1, 1), (0, 3), (0, 1), (0, 2), (1, 2)]
                for a, rel in order:
                    gx = lax.rem(x + rel, NX)
                    for l in range(LH):
                        pltpu.make_async_copy(
                            kernels.at[a * LH + l, :, pl.ds(pl.multiple_of(gx * (NZ * SRC), 128), NZ * SRC)],
                            kb.at[a * NX + rel, :, pl.ds(l * NZ * SRC, NZ * SRC)],
                            ksem.at[a * NX + rel, l],
                        ).start()
                pltpu.make_async_copy(incident, inc, lsem.at[3]).start()
                pltpu.make_async_copy(tiles, tl, lsem.at[4]).start()

        @at(t0 + 1.2 * u)
        def _():
            for a in range(2):
                p = axis(a, 0)
                relay(h, a, (0, 0), 0, p)
            for a in range(2):
                p = axis(a, 0)
                spread(h, a, neg(p), 2)
                spread(h, a, p, 3)

        @at(t0 + 2.2 * u)
        def _():
            for a in range(2):
                relay(h, a, (0, 0), 1, axis(a, 1))

        @at(t0 + 2.7 * u)
        def _():
            for a in range(2):
                p = axis(a, 0)
                far(h, a, (0, 0), 0, p)
                spread(h, a, mul(p, 2), 4)
            for a in range(2):
                wait(piece(h, a, 0, 0), hsem.at[h, a])
            mm(h, 1, 0)

        @at(t0 + 3.7 * u)
        def _():
            for a in range(2):
                relay(h, a, neg(axis(a, 0)), 2, axis(a, 1))

        @at(t0 + 4.7 * u)
        def _():
            for a in range(2):
                relay(h, a, axis(a, 0), 3, axis(a, 1))

        @at(t0 + 5.2 * u)
        def _():
            for a in range(2):
                far(h, a, (0, 0), 1, axis(a, 1))
            mm(h, 0, 0)

        @at(t0 + 6.2 * u)
        def _():
            for a in range(2):
                relay(h, a, mul(axis(a, 0), 2), 4, axis(a, 1))

        @at(t0 + 6.3 * u)
        def _():
            mm(h, 1, -1)

        @at(t0 + 6.5 * u)
        def _():
            mm(h, 1, 1)

        @at(t0 + 6.8 * u)
        def _():
            for a in range(2):
                far(h, a, neg(axis(a, 0)), 2, axis(a, 1))
            mm(h, 0, -1)

        @at(t0 + 7.3 * u)
        def _():
            for a in range(2):
                far(h, a, axis(a, 0), 3, axis(a, 1))
            mm(h, 0, 1)

        @at(t0 + 7.8 * u)
        def _():
            for a in range(2):
                far(h, a, mul(axis(a, 0), 2), 4, axis(a, 1))
            mm(h, 0, 2)
            mm(h, 1, 2)

    tab = {}

    def position(r):
        p = jnp.int32(0)
        for b in range(NY * 2):
            p = p + jnp.where(owner_s[col * (NY * 2) + b] == r, b, 0)
        return jnp.minimum(p, NY * 2 - 1)

    def summed(h, t0, gap):
        hh = CL // 2

        @at(t0)
        def _():
            if "pos" not in tab:
                wait(owner_s, lsem.at[0])
                tab["pos"] = {dy: position(at_row(dy)) for dy in (0, 1, 2, 3)}
                tab["oth"] = {dy: position(at_row(dy) + other - core) for dy in (0, 1, 2, 3)}
            for i, dy in enumerate((2, 1, 3, 0)):
                sp[h, i] = acc[h, tab["oth"][dy]]
                send(sp.at[h, i], rp.at[h, i], psend.at[h], psem.at[h, i], y * 2 + other, col)

        @at(t0 + gap)
        def _():
            wait(rp.at[h, 0], psem.at[h, 0])
            ts[h, 0] = acc[h, tab["pos"][2]] + rp[h, 0]
            send(ts.at[h, 0, pl.ds(0, hh)], rf.at[h, 0], ysend.at[h], ysem.at[h, 0], at_row(1), col)
            send(ts.at[h, 0, pl.ds(hh, hh)], rf.at[h, 1], ysend.at[h], ysem.at[h, 1], at_row(-1), col)
            wait(rp.at[h, 1], psem.at[h, 1])
            ts[h, 1] = acc[h, tab["pos"][1]] + rp[h, 1]
            send(ts.at[h, 1, pl.ds(hh, hh)], ry.at[h, 0, pl.ds(hh, hh)], ysend.at[h], ysem.at[h, 2], at_row(1), col)
            wait(rp.at[h, 2], psem.at[h, 2])
            ts[h, 2] = acc[h, tab["pos"][3]] + rp[h, 2]
            send(ts.at[h, 2, pl.ds(0, hh)], ry.at[h, 1, pl.ds(0, hh)], ysend.at[h], ysem.at[h, 3], at_row(-1), col)
            wait(rp.at[h, 3], psem.at[h, 3])
            if h == 0:
                wait(inc, lsem.at[3])
            drv[h] = inc[0, :, pl.ds(h * W, W)] - (acc[h, tab["pos"][0]] + rp[h, 3])

        @at(t0 + 2 * gap)
        def _():
            wait(rf.at[h, 0], ysem.at[h, 0])
            ts[h, 1, pl.ds(0, hh)] += rf[h, 0]
            send(ts.at[h, 1, pl.ds(0, hh)], ry.at[h, 0, pl.ds(0, hh)], ysend.at[h], ysem.at[h, 4], at_row(1), col)
            wait(rf.at[h, 1], ysem.at[h, 1])
            ts[h, 2, pl.ds(hh, hh)] += rf[h, 1]
            send(ts.at[h, 2, pl.ds(hh, hh)], ry.at[h, 1, pl.ds(hh, hh)], ysend.at[h], ysem.at[h, 5], at_row(-1), col)

        @at(t0 + 3 * gap)
        def _():
            wait(ry.at[h, 0, pl.ds(hh, hh)], ysem.at[h, 2])
            wait(ry.at[h, 1, pl.ds(0, hh)], ysem.at[h, 3])
            wait(ry.at[h, 0, pl.ds(0, hh)], ysem.at[h, 4])
            wait(ry.at[h, 1, pl.ds(hh, hh)], ysem.at[h, 5])
            drv[h] = drv[h] - (ry[h, 0] + ry[h, 1])

    def slots():
        if "slots" not in tab:
            wait(pairs_s, lsem.at[1])
            made = []
            for t in range(TILES):
                s = jnp.clip(pairs_s[1, t], 0, CL - 1)
                zi = jnp.minimum(lax.rem(lax.shift_right_logical(s, 3) - col + 2 * NX * NZ + 1, NX * NZ), 2)
                made.append((zi, jnp.clip(owner_s[s], 0, 2 * NY - 1)))
            tab["slots"] = made
        return tab["slots"]

    @at(3.0)
    def _():
        wait(tl, lsem.at[4])
        wait(counts_s, lsem.at[2])
        for t in range(TILES):
            tcat[:, pl.ds(t * CL, CL)] = jnp.where(t < counts_s[0], tl[t], jnp.zeros((), BF16))

    def sweep(h, s, t0, gap):
        g = gat[h][s]
        up, down, over = at_row(1), at_row(-1), at_row(2)
        hh = CL // 2

        @at(t0)
        def _():
            cur = drv[h] if s == 0 else den[h]
            g[1, row] = cur.astype(BF16)
            src = g.at[1, row]
            for dc, zi in ((1, 0), (-1, 2), (0, 1)):
                send(src, g.at[zi, row], ssend.at[h, s, 0], ssem.at[h, s, 1], up, near_col(dc))
                send(src, g.at[zi, row], ssend.at[h, s, 0], ssem.at[h, s, 2], down, near_col(dc))
            for dc, zi in ((1, 0), (-1, 2)):
                send(src, g.at[zi, row], ssend.at[h, s, 0], ssem.at[h, s, 0], row, near_col(dc))

        def cross(r, i):
            send(g.at[:, r], g.at[:, r], ssend.at[h, s, 1], ssem.at[h, s, i], y * 2 + other, col)

        @at(t0 + gap)
        def _():
            wait(g.at[:, down], ssem.at[h, s, 1])
            send(g.at[:, down, pl.ds(0, hh)], g.at[:, down, pl.ds(0, hh)], ssend.at[h, s, 1], ssem.at[h, s, 3], up, col)
            wait(g.at[:, up], ssem.at[h, s, 2])
            send(g.at[:, up, pl.ds(hh, hh)], g.at[:, up, pl.ds(hh, hh)], ssend.at[h, s, 1], ssem.at[h, s, 4], down, col)
            wait(g.at[pl.ds(0, 2), row], ssem.at[h, s, 0])
            cross(row, 5)
            cross(down, 6)
            cross(up, 7)

        @at(t0 + 2 * gap)
        def _():
            wait(g.at[:, over, pl.ds(0, hh)], ssem.at[h, s, 3])
            wait(g.at[:, over, pl.ds(hh, hh)], ssem.at[h, s, 4])
            cross(over, 8)

        @at(t0 + 3 * gap)
        def _():
            for i, r in ((5, row), (6, down), (7, up), (8, over)):
                wait(g.at[:, r + other - core], ssem.at[h, s, i])
            picked = jnp.concatenate([g[zi, r] for zi, r in slots()], axis=0)
            near = jnp.dot(tcat[...], picked, preferred_element_type=F32)
            d = drv[h]
            cur = d if s == 0 else den[h]
            den[h] = cur + DAMPING * (d - cur - near)
            if s == SWEEPS - 1:
                pltpu.make_async_copy(den.at[h], out.at[0, :, pl.ds(h * W, W)], osem.at[h]).start()

    U = 1.5
    T1 = 7.6
    gather(0, 0.0, U)
    summed(0, 13.0, 1.4)
    for s in range(SWEEPS):
        sweep(0, s, 17.5 + 4.6 * s, 1.5)
    gather(1, T1, U)
    summed(1, T1 + 14.0, 1.4)
    for s in range(SWEEPS):
        sweep(1, s, T1 + 18.3 + 4.6 * s, 1.5)

    for _, _, f in sorted(events, key=lambda e: e[:2]):
        f()

    for h in range(HALVES):
        for d in range(2):
            wait(hb.at[h, :, pl.ds(0, 3), :, pl.ds(0, 240), :], gsend.at[h, d])
        wait(sp.at[h], psend.at[h])
        wait(ts.at[h], ysend.at[h])
        for s in range(SWEEPS):
            wait(gat[h][s].at[0], ssend.at[h, s, 0])
            wait(gat[h][s].at[:, pl.ds(0, 5)], ssend.at[h, s, 1])
    for h in range(HALVES):
        wait(den.at[h], osem.at[h])


def per_device(kernels, history, incident, owner, pairs, tiles, counts):
    dma = pltpu.SemaphoreType.DMA
    any_ = pl.BlockSpec(memory_space=pl.ANY)
    return pl.pallas_call(
        body,
        out_shape=jax.ShapeDtypeStruct(incident.shape, F32),
        in_specs=[any_] * 7,
        out_specs=any_,
        scratch_shapes=[
            pltpu.VMEM((HALVES, 2, NX, LH, NZ * SRC, W), BF16),
            pltpu.VMEM((2 * NX, 8 * CL, DEPTH), BF16),
            pltpu.VMEM((HALVES, 8, CL, W), F32),
            pltpu.VMEM((HALVES, 4, CL, W), F32),
            pltpu.VMEM((HALVES, 4, CL, W), F32),
            pltpu.VMEM((HALVES, 3, CL, W), F32),
            pltpu.VMEM((HALVES, 2, CL // 2, W), F32),
            pltpu.VMEM((HALVES, 2, CL, W), F32),
            pltpu.VMEM((1, CL, COLS), F32),
            pltpu.VMEM((HALVES, CL, W), F32),
            pltpu.VMEM((HALVES, CL, W), F32),
            pltpu.VMEM((TILES, CL, CL), BF16),
            pltpu.VMEM((CL, TILES * CL), BF16),
            *[pltpu.VMEM((3, 8, CL, W), BF16)] * (HALVES * SWEEPS),
            pltpu.SMEM((128,), jnp.int32),
            pltpu.SMEM((2, TILES), jnp.int32),
            pltpu.SMEM((1,), jnp.int32),
            dma((5,)), dma((8, LH)), dma((HALVES, 2)), dma((HALVES, 2, 5, 4)), dma((HALVES, 2)),
            dma((HALVES, 4)), dma((HALVES,)), dma((HALVES, 6)), dma((HALVES,)),
            dma((HALVES, SWEEPS, 9)), dma((HALVES, SWEEPS, 2)), dma((HALVES,)),
        ],
        compiler_params=pltpu.CompilerParams(
            collective_id=0, has_side_effects=True, vmem_limit_bytes=56 * 2**20
        ),
        cost_estimate=pl.CostEstimate(flops=5_200_000_000, bytes_accessed=21_000_000, transcendentals=0),
    )(kernels, history, incident, owner, pairs.T, tiles, counts)


def solution(mesh):
    both = ("row", "col")
    in_specs = (
        P(None, "col", "row"), P(None, both, None), P(both, None, None), P(),
        P(both, None), P(both, None, None), P(both),
    )
    return jax.shard_map(
        per_device, mesh=mesh, in_specs=in_specs, out_specs=P(both, None, None), check_vma=False
    )
```

```python
import functools

import jax
import jax.numpy as jnp
from jax import lax
from jax.experimental import pallas as pl
from jax.experimental.pallas import tpu as pltpu
from jax.sharding import PartitionSpec as P

MESH = pl.DeviceIdType.MESH
F32, BF16 = jnp.float32, jnp.bfloat16

SWEEPS = 3
DAMPING = 0.7

NX, NZ, NY = 4, 4, 4
LAGS, SRC, COLS, CL = 6, 96, 256, 128
HALVES = 2
W = COLS // HALVES
LH = LAGS // 2
DEPTH = LH * NZ * SRC
TILES = 12


def body(kernels, history, incident, owner, pairs, tiles, counts, out,
         hb, kb, acc, mine, sp, rp, ts, ry, inc, drv, den, fin, last, tl, wt,
         gat00, gat01, gat02, gat10, gat11, gat12, owner_s, pairs_s, counts_s, codes,
         lsem, ksem, hsem, gsem, gsend, bsem, bsend, psem, psend, ysem, ysend, ssem, ssend, fsem, fsend, osem):
    row, col = lax.axis_index("row"), lax.axis_index("col")
    y, core = lax.div(row, 2), lax.rem(row, 2)
    x, z = lax.div(col, NZ), lax.rem(col, NZ)
    other = 1 - core

    def at_col(dx, dz):
        return lax.rem(x + dx + NX, NX) * NZ + lax.rem(z + dz + NZ, NZ)

    def at_row(dy):
        return lax.rem(y + dy + NY, NY) * 2 + core

    def near_col(dc):
        return lax.rem(col + dc + NX * NZ, NX * NZ)

    def send(src, dst, ssem_, rsem_, r, c):
        pltpu.make_async_remote_copy(
            src_ref=src, dst_ref=dst, send_sem=ssem_, recv_sem=rsem_,
            device_id={"row": r, "col": c}, device_id_type=MESH,
        ).start()

    def wait(ref, sem):
        pltpu.make_async_copy(ref, ref, sem).wait()

    gat = ((gat00, gat01, gat02), (gat10, gat11, gat12))

    barrier = pltpu.get_barrier_semaphore()
    greet = [(row, at_col(1, 0)), (row, at_col(-1, 0)), (row, at_col(0, 1)), (row, at_col(0, -1))]
    greet += [(at_row(1), col), (at_row(-1), col), (at_row(2), col), (y * 2 + other, col)]
    for r, c in greet:
        pl.semaphore_signal(barrier, inc=1, device_id={"row": r, "col": c}, device_id_type=MESH)

    def piece(h, a, dx, dz, lo=0, n=SRC):
        zr = pl.multiple_of(lax.rem(z + dz + NZ, NZ) * SRC + lo, 16)
        return hb.at[h, a, dx % NX, :, pl.ds(zr, n), :]

    def own(h, a):
        return history.at[pl.ds(a * LH, LH), :, pl.ds(h * W, W)]

    for h in range(HALVES):
        for a in range(2):
            pltpu.make_async_copy(own(h, a), piece(h, a, 0, 0), hsem.at[h, a]).start()
    pltpu.make_async_copy(owner, owner_s, lsem.at[0]).start()
    pltpu.make_async_copy(pairs, pairs_s, lsem.at[1]).start()
    pltpu.make_async_copy(counts, counts_s, lsem.at[2]).start()
    pl.semaphore_wait(barrier, len(greet))
    mate = y * 2 + other

    events = []

    def at(t):
        def add(f):
            events.append((t, len(events), f))
        return add

    def axis(a, phase):
        return ((1, 0), (0, 1))[(a + phase) % 2]

    def move(h, a, off, d, lo, n, sem, first=False):
        src = own(h, a) if first else piece(h, a, off[0], off[1], lo, n)
        zr = pl.multiple_of(lax.rem(z + off[1] + NZ, NZ) * SRC + lo, 16)
        dst = hb.at[h, a, (off[0] - d[0]) % NX, :, pl.ds(zr, n), :]
        send(src, dst, gsend.at[h, 0 if d[0] else 1], sem, row, at_col(d[0], d[1]))

    def neg(d):
        return (-d[0], -d[1])

    def mul(d, k):
        return (d[0] * k, d[1] * k)

    def add2(p, q):
        return (p[0] + q[0], p[1] + q[1])

    half = SRC // 2

    def spread(h, a, off, j, first=False):
        d = axis(a, 1)
        move(h, a, off, d, 0, SRC, gsem.at[h, a, j, 0], first)
        move(h, a, off, neg(d), 0, SRC, gsem.at[h, a, j, 1], first)

    def relay(h, a, off, j, d):
        lo, hi = add2(off, neg(d)), add2(off, d)
        wait(piece(h, a, *lo), gsem.at[h, a, j, 0])
        move(h, a, lo, d, 0, half, gsem.at[h, a, j, 2])
        wait(piece(h, a, *hi), gsem.at[h, a, j, 1])
        move(h, a, hi, neg(d), half, half, gsem.at[h, a, j, 3])

    def far(h, a, off, j, d):
        o = add2(off, mul(d, 2))
        wait(piece(h, a, o[0], o[1], 0, half), gsem.at[h, a, j, 2])
        wait(piece(h, a, o[0], o[1], half, half), gsem.at[h, a, j, 3])

    order = [(1, 0), (0, 0), (1, 3), (1, 1), (0, 3), (0, 1), (1, 2), (0, 2)]

    def mm(a, dx):
        g = a * NX + dx % NX
        for l in range(LH):
            wait(kb.at[g, :, pl.ds(l * NZ * SRC, NZ * SRC)], ksem.at[g, l])
        w = jnp.concatenate([hb[h, a, dx % NX].reshape(DEPTH, W) for h in range(HALVES)], axis=1)
        d = jnp.dot(kb[g], w, preferred_element_type=F32)
        for h in range(HALVES):
            part = d[:, h * W:(h + 1) * W].reshape(2 * NY, CL, W)
            acc[h] = part if (a, dx % NX) == order[0] else acc[h] + part

    def product(h, t0, a, dx):
        if h == HALVES - 1:
            @at(t0)
            def _():
                mm(a, dx)

    def gather(h, t0, u):
        @at(t0)
        def _():
            for a in range(2):
                d = axis(a, 0)
                move(h, a, (0, 0), d, 0, SRC, gsem.at[h, a, 0, 0], True)
                move(h, a, (0, 0), neg(d), 0, SRC, gsem.at[h, a, 0, 1], True)
            for a in range(2):
                spread(h, a, (0, 0), 1, True)

        @at(t0 + 1.2 * u)
        def _():
            for a in range(2):
                p = axis(a, 0)
                relay(h, a, (0, 0), 0, p)
            for a in range(2):
                p = axis(a, 0)
                spread(h, a, neg(p), 2)
                spread(h, a, p, 3)

        @at(t0 + 2.2 * u)
        def _():
            for a in range(2):
                relay(h, a, (0, 0), 1, axis(a, 1))

        @at(t0 + 2.7 * u)
        def _():
            for a in range(2):
                p = axis(a, 0)
                far(h, a, (0, 0), 0, p)
                spread(h, a, mul(p, 2), 4)
            for a in range(2):
                wait(piece(h, a, 0, 0), hsem.at[h, a])

        product(h, t0 + 2.7 * u, 1, 0)

        @at(t0 + 3.7 * u)
        def _():
            for a in range(2):
                relay(h, a, neg(axis(a, 0)), 2, axis(a, 1))

        @at(t0 + 4.7 * u)
        def _():
            for a in range(2):
                relay(h, a, axis(a, 0), 3, axis(a, 1))

        @at(t0 + 5.2 * u)
        def _():
            for a in range(2):
                far(h, a, (0, 0), 1, axis(a, 1))

        product(h, t0 + 5.2 * u, 0, 0)

        @at(t0 + 6.2 * u)
        def _():
            for a in range(2):
                relay(h, a, mul(axis(a, 0), 2), 4, axis(a, 1))

        product(h, t0 + 6.3 * u, 1, -1)

        product(h, t0 + 6.5 * u, 1, 1)

        @at(t0 + 6.8 * u)
        def _():
            for a in range(2):
                far(h, a, neg(axis(a, 0)), 2, axis(a, 1))

        product(h, t0 + 6.8 * u, 0, -1)

        @at(t0 + 7.3 * u)
        def _():
            for a in range(2):
                far(h, a, axis(a, 0), 3, axis(a, 1))

        product(h, t0 + 7.3 * u, 0, 1)

        @at(t0 + 7.8 * u)
        def _():
            far(h, 1, mul(axis(1, 0), 2), 4, axis(1, 1))

        product(h, t0 + 7.8 * u, 1, 2)

        @at(t0 + 7.8 * u)
        def _():
            far(h, 0, mul(axis(0, 0), 2), 4, axis(0, 1))

        product(h, t0 + 7.8 * u, 0, 2)

    tab = {}

    def position(r):
        p = jnp.int32(0)
        for b in range(NY * 2):
            p = p + jnp.where(owner_s[col * (NY * 2) + b] == r, b, 0)
        return jnp.minimum(p, NY * 2 - 1)

    low = lax.broadcasted_iota(jnp.int32, (CL, W), 1) < W // 2

    def pack(a, b):
        ra, rb = pltpu.roll(a, W // 2, 1), pltpu.roll(b, W // 2, 1)
        lo, hi = jnp.where(low, a, rb), jnp.where(low, ra, b)
        return jnp.where(core == 0, lo, hi), jnp.where(core == 0, hi, lo)

    def summed(h, t0, t1, t2):
        @at(t0)
        def _():
            if "pos" not in tab:
                tab["pos"] = {(dy, q): position(at_row(dy) - core + q) for dy in range(NY) for q in (0, 1)}
            for i, dy in enumerate((2, 1, 3, 0)):
                own_, theirs = pack(acc[h, tab["pos"][dy, 0]], acc[h, tab["pos"][dy, 1]])
                sp[h, i] = theirs
                send(sp.at[h, i], rp.at[h, i], psend.at[h], psem.at[h, i], mate, col)
                mine[h, i] = own_

        @at(t1)
        def _():
            for i, dy in enumerate((2, 1, 3)):
                wait(rp.at[h, i], psem.at[h, i])
                ts[h, i] = mine[h, i] + rp[h, i]
                send(ts.at[h, i], ry.at[h, i], ysend.at[h], ysem.at[h, i], at_row(dy), col)
            wait(rp.at[h, 3], psem.at[h, 3])
            if h == 0:
                wait(inc.at[core], lsem.at[3])
                wait(inc.at[other], bsem.at[0])
            cols = pl.ds(h * W, W)
            drv[h] = pack(inc[0, 0, :, cols], inc[1, 0, :, cols])[0] - (mine[h, 3] + rp[h, 3])

        @at(t2)
        def _():
            for i in (1, 2, 0):
                wait(ry.at[h, i], ysem.at[h, i])
            drv[h] = drv[h] - (ry[h, 0] + (ry[h, 1] + ry[h, 2]))

    @at(1.0)
    def _():
        wait(owner_s, lsem.at[0])
        wait(pairs_s, lsem.at[1])
        wait(counts_s, lsem.at[2])
        for t in range(TILES):
            s = jnp.clip(pairs_s[1, t], 0, CL - 1)
            zi = jnp.minimum(lax.rem(lax.shift_right_logical(s, 3) - col + 2 * NX * NZ + 1, NX * NZ), 2)
            codes[core, t] = jnp.where(t < counts_s[0], zi * (2 * NY) + owner_s[s], -1)
        for t in range(TILES, 16):
            codes[core, t] = -1
        send(codes.at[core], codes.at[core], bsend.at[2], bsem.at[2], mate, col)

    def weights(dy, t0):
        @at(t0)
        def _():
            if dy == 0:
                wait(codes.at[other], bsem.at[2])
                wait(tl.at[core], lsem.at[4])
                wait(tl.at[other], bsem.at[1])
            for k in range(2):
                c = [codes[k, t] for t in range(TILES)]
                for zi in range(3):
                    for q in range(2):
                        want = zi * (2 * NY) + at_row(dy) - core + q
                        found = jnp.int32(-1)
                        for t in range(TILES):
                            found = jnp.where(c[t] == want, t, found)
                        tile = tl[k, jnp.maximum(found, 0)]
                        wt[dy, pl.ds((k * 2 + q) * CL, CL), pl.ds(zi * CL, CL)] = jnp.where(
                            found >= 0, tile, jnp.zeros((), BF16))

    for dy in range(NY):
        weights(dy, 4.0 + 0.9 * dy)

    def sweep(h, s, t0, t1):
        g = gat[h][s]
        ys = [lax.rem(y + dy, NY) for dy in range(NY)]

        @at(t0)
        def _():
            cur = drv[h] if s == 0 else den[h]
            g[y, 1] = cur.astype(BF16)
            src = g.at[y, 1]
            for i in (2, 1, 3, 0):
                for dc, zi in ((1, 0), (-1, 2), (0, 1)):
                    if i or dc:
                        send(src, g.at[y, zi], ssend.at[h, s], ssem.at[h, s, i], at_row(-i), near_col(dc))

        @at(t1)
        def _():
            near = None
            for i in (0, 1, 3, 2):
                if i:
                    wait(g.at[ys[i]], ssem.at[h, s, i])
                else:
                    wait(g.at[y, pl.ds(0, 2)], ssem.at[h, s, 0])
                part = jnp.dot(wt[i], g[ys[i]].reshape(3 * CL, W), preferred_element_type=F32)
                near = part if near is None else near + part
            n00, n01, n10, n11 = (near[q * CL:(q + 1) * CL] for q in range(4))
            near = jnp.where(low, n00 + pltpu.roll(n01, W // 2, 1), pltpu.roll(n10, W // 2, 1) + n11)
            d = drv[h]
            cur = d if s == 0 else den[h]
            new = cur + DAMPING * (d - cur - near)
            if s < SWEEPS - 1:
                den[h] = new
            else:
                fin[h] = new
                send(fin.at[h], last.at[h], fsend.at[h], fsem.at[h], mate, col)

    def finish(h, t0):
        @at(t0)
        def _():
            wait(last.at[h], fsem.at[h])
            mine_, theirs = fin[h], pltpu.roll(last[h], W // 2, 1)
            den[h] = jnp.where(
                core == 0, jnp.where(low, mine_, theirs), jnp.where(low, theirs, mine_))
            pltpu.make_async_copy(den.at[h], out.at[0, :, pl.ds(h * W, W)], osem.at[h]).start()

    def loads():
        for a, rel in order:
            gx = lax.rem(x + rel, NX)
            for l in range(LH):
                pltpu.make_async_copy(
                    kernels.at[a * LH + l, :, pl.ds(pl.multiple_of(gx * (NZ * SRC), 128), NZ * SRC)],
                    kb.at[a * NX + rel, :, pl.ds(l * NZ * SRC, NZ * SRC)],
                    ksem.at[a * NX + rel, l],
                ).start()
        pltpu.make_async_copy(incident, inc.at[core], lsem.at[3]).start()
        pltpu.make_async_copy(tiles, tl.at[core], lsem.at[4]).start()
        send(incident, inc.at[core], bsend.at[0], bsem.at[0], mate, col)
        send(tiles, tl.at[core], bsend.at[1], bsem.at[1], mate, col)

    events.append((0.02, 1000, loads))

    gather(0, 0.0, 3.2)
    gather(1, 0.01, 3.2)
    summed(0, 30.0, 31.4, 36.5)
    summed(1, 30.1, 31.5, 38.5)
    ST0 = (36.6, 44.0, 51.5, 59.0)
    ST1 = (38.6, 46.0, 53.5, 61.0)
    for s in range(SWEEPS):
        sweep(0, s, ST0[s], ST0[s + 1] - 0.05)
        sweep(1, s, ST1[s], ST1[s + 1] - 0.05)
    finish(0, 60.0)
    finish(1, 62.0)

    for _, _, f in sorted(events, key=lambda e: e[:2]):
        f()

    wait(inc.at[core], bsend.at[0])
    wait(tl.at[core], bsend.at[1])
    wait(codes.at[core], bsend.at[2])
    for h in range(HALVES):
        for d in range(2):
            wait(hb.at[h, :, pl.ds(0, 3), :, pl.ds(0, 240), :], gsend.at[h, d])
        wait(sp.at[h], psend.at[h])
        wait(ts.at[h], ysend.at[h])
        for s in range(SWEEPS):
            wait(tl.at[0, pl.ds(0, NY * 3 - 1)], ssend.at[h, s])
        wait(fin.at[h], fsend.at[h])
        wait(den.at[h], osem.at[h])


def per_device(kernels, history, incident, owner, pairs, tiles, counts):
    dma = pltpu.SemaphoreType.DMA
    any_ = pl.BlockSpec(memory_space=pl.ANY)
    return pl.pallas_call(
        body,
        out_shape=jax.ShapeDtypeStruct(incident.shape, F32),
        in_specs=[any_] * 7,
        out_specs=any_,
        scratch_shapes=[
            pltpu.VMEM((HALVES, 2, NX, LH, NZ * SRC, W), BF16),
            pltpu.VMEM((2 * NX, 8 * CL, DEPTH), BF16),
            pltpu.VMEM((HALVES, 8, CL, W), F32),
            *[pltpu.VMEM((HALVES, 4, CL, W), F32)] * 3,
            *[pltpu.VMEM((HALVES, 3, CL, W), F32)] * 2,
            pltpu.VMEM((2, 1, CL, COLS), F32),
            *[pltpu.VMEM((HALVES, CL, W), F32)] * 4,
            pltpu.VMEM((2, TILES, CL, CL), BF16),
            pltpu.VMEM((NY, 4 * CL, 3 * CL), BF16),
            *[pltpu.VMEM((NY, 3, CL, W), BF16)] * (HALVES * SWEEPS),
            pltpu.SMEM((128,), jnp.int32),
            pltpu.SMEM((2, TILES), jnp.int32),
            pltpu.SMEM((1,), jnp.int32),
            pltpu.SMEM((2, 16), jnp.int32),
            dma((5,)), dma((8, LH)), dma((HALVES, 2)), dma((HALVES, 2, 5, 4)), dma((HALVES, 2)),
            dma((3,)), dma((3,)), dma((HALVES, 4)), dma((HALVES,)), dma((HALVES, 3)), dma((HALVES,)),
            dma((HALVES, SWEEPS, 4)), dma((HALVES, SWEEPS)), dma((HALVES,)), dma((HALVES,)), dma((HALVES,)),
        ],
        compiler_params=pltpu.CompilerParams(
            collective_id=0, has_side_effects=True, vmem_limit_bytes=56 * 2**20
        ),
        cost_estimate=pl.CostEstimate(flops=5_200_000_000, bytes_accessed=21_000_000, transcendentals=0),
    )(kernels, history, incident, owner, pairs.T, tiles, counts)


def solution(mesh):
    both = ("row", "col")
    in_specs = (
        P(None, "col", "row"), P(None, both, None), P(both, None, None), P(),
        P(both, None), P(both, None, None), P(both),
    )
    return jax.shard_map(
        per_device, mesh=mesh, in_specs=in_specs, out_specs=P(both, None, None), check_vma=False
    )
```

```python
import functools

import jax
import jax.numpy as jnp
from jax import lax
from jax.experimental import pallas as pl
from jax.experimental.pallas import tpu as pltpu
from jax.sharding import PartitionSpec as P

MESH = pl.DeviceIdType.MESH
F32, BF16 = jnp.float32, jnp.bfloat16

SWEEPS = 3
DAMPING = 0.7

NX, NZ, NY = 4, 4, 4
LAGS, SRC, COLS, CL = 6, 96, 256, 128
HALVES = 2
W = COLS // HALVES
CW = COLS // 8
LH = LAGS // 2
DEPTH = LH * NZ * SRC
TILES = 12


def body(kernels, history, incident, owner, pairs, tiles, counts, out,
         hb, kb, acc, mine, sp, rp, ts, ry, inc, ict, icd, drv, den, fin, last, res, tl,
         gat0, gat1, gat2, owner_s, pairs_s, counts_s, codes,
         lsem, ksem, hsem, gsem, gsend, tsem, tsend, isem, isend, csem, csend,
         psem, psend, ysem, ysend, ssem, ssend, fsem, fsend, osem):
    row, col = lax.axis_index("row"), lax.axis_index("col")
    y, core = lax.div(row, 2), lax.rem(row, 2)
    x, z = lax.div(col, NZ), lax.rem(col, NZ)
    other = 1 - core

    def at_col(dx, dz):
        return lax.rem(x + dx + NX, NX) * NZ + lax.rem(z + dz + NZ, NZ)

    def at_row(dy):
        return lax.rem(y + dy + NY, NY) * 2 + core

    def near_col(dc):
        return lax.rem(col + dc + NX * NZ, NX * NZ)

    def send(src, dst, ssem_, rsem_, r, c):
        pltpu.make_async_remote_copy(
            src_ref=src, dst_ref=dst, send_sem=ssem_, recv_sem=rsem_,
            device_id={"row": r, "col": c}, device_id_type=MESH,
        ).start()

    def wait(ref, sem):
        pltpu.make_async_copy(ref, ref, sem).wait()

    gat = (gat0, gat1, gat2)

    barrier = pltpu.get_barrier_semaphore()
    greet = [(row, at_col(1, 0)), (row, at_col(-1, 0)), (row, at_col(0, 1)), (row, at_col(0, -1))]
    greet += [(at_row(1), col), (at_row(-1), col), (at_row(2), col), (y * 2 + other, col)]
    for r, c in greet:
        pl.semaphore_signal(barrier, inc=1, device_id={"row": r, "col": c}, device_id_type=MESH)

    def piece(h, a, dx, dz, lo=0, n=SRC):
        zr = pl.multiple_of(lax.rem(z + dz + NZ, NZ) * SRC + lo, 16)
        return hb.at[h, a, dx % NX, :, pl.ds(zr, n), :]

    def own(h, a):
        return history.at[pl.ds(a * LH, LH), :, pl.ds(h * W, W)]

    for h in range(HALVES):
        for a in range(2):
            pltpu.make_async_copy(own(h, a), piece(h, a, 0, 0), hsem.at[h, a]).start()
    pltpu.make_async_copy(owner, owner_s, lsem.at[0]).start()
    pltpu.make_async_copy(pairs, pairs_s, lsem.at[1]).start()
    pltpu.make_async_copy(counts, counts_s, lsem.at[2]).start()
    pl.semaphore_wait(barrier, len(greet))

    events = []

    def at(t):
        def add(f):
            events.append((t, len(events), f))
        return add

    def axis(a, phase):
        return ((1, 0), (0, 1))[(a + phase) % 2]

    def move(h, a, off, d, lo, n, sem, first=False):
        src = own(h, a) if first else piece(h, a, off[0], off[1], lo, n)
        zr = pl.multiple_of(lax.rem(z + off[1] + NZ, NZ) * SRC + lo, 16)
        dst = hb.at[h, a, (off[0] - d[0]) % NX, :, pl.ds(zr, n), :]
        send(src, dst, gsend.at[h, 0 if d[0] else 1], sem, row, at_col(d[0], d[1]))

    def neg(d):
        return (-d[0], -d[1])

    def mul(d, k):
        return (d[0] * k, d[1] * k)

    def add2(p, q):
        return (p[0] + q[0], p[1] + q[1])

    half = SRC // 2

    def spread(h, a, off, j, first=False):
        d = axis(a, 1)
        move(h, a, off, d, 0, SRC, gsem.at[h, a, j, 0], first)
        move(h, a, off, neg(d), 0, SRC, gsem.at[h, a, j, 1], first)

    def relay(h, a, off, j, d):
        lo, hi = add2(off, neg(d)), add2(off, d)
        wait(piece(h, a, *lo), gsem.at[h, a, j, 0])
        move(h, a, lo, d, 0, half, gsem.at[h, a, j, 2])
        wait(piece(h, a, *hi), gsem.at[h, a, j, 1])
        move(h, a, hi, neg(d), half, half, gsem.at[h, a, j, 3])

    def far(h, a, off, j, d):
        o = add2(off, mul(d, 2))
        wait(piece(h, a, o[0], o[1], 0, half), gsem.at[h, a, j, 2])
        wait(piece(h, a, o[0], o[1], half, half), gsem.at[h, a, j, 3])

    order = [(1, 0), (0, 0), (1, 3), (1, 1), (0, 3), (0, 1), (1, 2), (0, 2)]

    def mm(a, dx):
        g = a * NX + dx % NX
        for l in range(LH):
            wait(kb.at[g, :, pl.ds(l * NZ * SRC, NZ * SRC)], ksem.at[g, l])
        w = jnp.concatenate([hb[h, a, dx % NX].reshape(DEPTH, W) for h in range(HALVES)], axis=1)
        d = jnp.dot(kb[g], w, preferred_element_type=F32)
        for h in range(HALVES):
            part = d[:, h * W:(h + 1) * W].reshape(2 * NY, CL, W)
            acc[h] = part if (a, dx % NX) == order[0] else acc[h] + part

    def product(h, t0, a, dx):
        if h == HALVES - 1:
            @at(t0)
            def _():
                mm(a, dx)

    def gather(h, t0, u):
        @at(t0)
        def _():
            for a in range(2):
                d = axis(a, 0)
                move(h, a, (0, 0), d, 0, SRC, gsem.at[h, a, 0, 0], True)
                move(h, a, (0, 0), neg(d), 0, SRC, gsem.at[h, a, 0, 1], True)
            for a in range(2):
                spread(h, a, (0, 0), 1, True)

        @at(t0 + 1.2 * u)
        def _():
            for a in range(2):
                p = axis(a, 0)
                relay(h, a, (0, 0), 0, p)
            for a in range(2):
                p = axis(a, 0)
                spread(h, a, neg(p), 2)
                spread(h, a, p, 3)

        @at(t0 + 2.2 * u)
        def _():
            for a in range(2):
                relay(h, a, (0, 0), 1, axis(a, 1))

        @at(t0 + 2.7 * u)
        def _():
            for a in range(2):
                p = axis(a, 0)
                far(h, a, (0, 0), 0, p)
                spread(h, a, mul(p, 2), 4)
            for a in range(2):
                wait(piece(h, a, 0, 0), hsem.at[h, a])

        product(h, t0 + 2.7 * u, 1, 0)

        @at(t0 + 3.7 * u)
        def _():
            for a in range(2):
                relay(h, a, neg(axis(a, 0)), 2, axis(a, 1))

        @at(t0 + 4.7 * u)
        def _():
            for a in range(2):
                relay(h, a, axis(a, 0), 3, axis(a, 1))

        @at(t0 + 5.2 * u)
        def _():
            for a in range(2):
                far(h, a, (0, 0), 1, axis(a, 1))

        product(h, t0 + 5.2 * u, 0, 0)

        @at(t0 + 6.2 * u)
        def _():
            for a in range(2):
                relay(h, a, mul(axis(a, 0), 2), 4, axis(a, 1))

        product(h, t0 + 6.3 * u, 1, -1)

        product(h, t0 + 6.5 * u, 1, 1)

        @at(t0 + 6.8 * u)
        def _():
            for a in range(2):
                far(h, a, neg(axis(a, 0)), 2, axis(a, 1))

        product(h, t0 + 6.8 * u, 0, -1)

        @at(t0 + 7.3 * u)
        def _():
            for a in range(2):
                far(h, a, axis(a, 0), 3, axis(a, 1))

        product(h, t0 + 7.3 * u, 0, 1)

        @at(t0 + 7.8 * u)
        def _():
            far(h, 1, mul(axis(1, 0), 2), 4, axis(1, 1))

        product(h, t0 + 7.8 * u, 1, 2)

        @at(t0 + 7.8 * u)
        def _():
            far(h, 0, mul(axis(0, 0), 2), 4, axis(0, 1))

        product(h, t0 + 7.8 * u, 0, 2)

    part = core * NY + y
    peers = [(dy, flip) for dy in (2, 1, 3) for flip in (0, 1)] + [(0, 1)]

    def peer(dy, flip):
        y2 = lax.rem(y + dy, NY)
        k2 = other if flip else core
        return y2 * 2 + k2, k2 * NY + y2

    def position(r):
        p = jnp.int32(0)
        for b in range(NY * 2):
            p = p + jnp.where(owner_s[col * (NY * 2) + b] == r, b, 0)
        return jnp.minimum(p, NY * 2 - 1)

    tab = {}

    @at(2.0)
    def _():
        wait(owner_s, lsem.at[0])
        wait(pairs_s, lsem.at[1])
        wait(counts_s, lsem.at[2])
        for t in range(TILES):
            s = jnp.clip(pairs_s[1, t], 0, CL - 1)
            zi = jnp.minimum(lax.rem(lax.shift_right_logical(s, 3) - col + 2 * NX * NZ + 1, NX * NZ), 2)
            codes[row, t] = jnp.where(t < counts_s[0], zi * (2 * NY) + owner_s[s], -1)
        for t in range(TILES, 16):
            codes[row, t] = -1
        wait(inc, lsem.at[3])
        for h in range(HALVES):
            ict[pl.ds(h * NY, NY)] = inc[0, :, h * W:(h + 1) * W].T.reshape(NY, CW, CL)
        icd[row] = ict[part]
        wait(tl.at[row], lsem.at[4])

    def exchange(t0):
        @at(t0)
        def _():
            for i, dy in enumerate((1, 3, 2)):
                r = peer(dy, 0)[0]
                wait(tl.at[r], tsem.at[i])
                send(tl.at[r], tl.at[r], tsend, tsem.at[4 + i], y * 2 + other, col)
            for i, (dy, flip) in enumerate(peers):
                r, p = peer(dy, flip)
                send(ict.at[p], icd.at[row], isend, isem.at[i], r, col)
                send(codes.at[row], codes.at[row], csend.at[i], csem.at[i], r, col)

    def back(dy):
        return (NY - dy) % NY

    def summed(t0, t1, t2):
        @at(t0)
        def _():
            pos = [position(jnp.int32(r)) for r in range(2 * NY)]
            for r in range(2 * NY):
                sp[r] = acc[other, pos[r]].T
                send(sp.at[r], rp.at[r], psend, psem.at[r], y * 2 + other, col)
            for r in range(2 * NY):
                mine[r] = acc[core, pos[r]].T

        @at(t1)
        def _():
            for g in range(2):
                for r in range(g * NY, g * NY + NY):
                    wait(rp.at[r], psem.at[r])
                    ts[r] = mine[r] + rp[r]
                for i, dy in enumerate((2, 1, 3)):
                    y2 = lax.rem(y + dy, NY)
                    send(ts.at[pl.ds(g * NY, NY), pl.ds(pl.multiple_of(y2 * CW, CW), CW)],
                         ry.at[i, pl.ds(g * NY, NY)], ysend, ysem.at[i, g], y2 * 2 + core, col)
            for i in range(7):
                dy, flip = peers[i]
                wait(icd.at[peer(back(dy), flip)[0]], isem.at[i])
            drv[...] = icd[...] - ts[:, pl.ds(pl.multiple_of(y * CW, CW), CW)]

        @at(t2)
        def _():
            for i in (1, 2, 0):
                for g in range(2):
                    wait(ry.at[i, pl.ds(g * NY, NY)], ysem.at[i, g])
            drv[...] = drv[...] - (ry[0] + (ry[1] + ry[2]))

    def sweep(s, t0, t1):
        g = gat[s]

        @at(t0)
        def _():
            if s == 0:
                for i, (dy, flip) in enumerate(peers):
                    wait(codes.at[peer(back(dy), flip)[0]], csem.at[i])
                for i, dy in enumerate((1, 3, 2)):
                    wait(tl.at[peer(dy, 1)[0]], tsem.at[4 + i])
                wait(tl.at[peer(0, 1)[0]], tsem.at[3])
            cur = drv[...] if s == 0 else den[...]
            g[1] = cur.astype(BF16)
            send(g.at[1], g.at[0], ssend.at[s], ssem.at[s, 0], row, near_col(1))
            send(g.at[1], g.at[2], ssend.at[s], ssem.at[s, 1], row, near_col(-1))

        @at(t1)
        def _():
            wait(g.at[0], ssem.at[s, 0])
            wait(g.at[2], ssem.at[s, 1])
            for r in range(2 * NY):
                blocks = []
                for t in range(TILES):
                    c = codes[r, t]
                    i = jnp.clip(c, 0, 6 * NY - 1)
                    u = g[lax.shift_right_logical(i, 3), lax.rem(i, 2 * NY)]
                    blocks.append(jnp.where(c >= 0, u, jnp.zeros((), BF16)))
                near = lax.dot_general(
                    jnp.concatenate(blocks, axis=1), jnp.concatenate([tl[r, t] for t in range(TILES)], axis=1),
                    (((1,), (1,)), ((), ())), preferred_element_type=F32)
                d = drv[r]
                cur = d if s == 0 else den[r]
                new = cur + DAMPING * (d - cur - near)
                if s < SWEEPS - 1:
                    den[r] = new
                else:
                    fin[r] = new
            if s == SWEEPS - 1:
                for i, (dy, flip) in enumerate(peers):
                    r = peer(dy, flip)[0]
                    send(fin.at[r], last.at[part], fsend, fsem.at[i], r, col)
                last[part] = fin[row]

    def finish(t0):
        @at(t0)
        def _():
            for i, (dy, flip) in enumerate(peers):
                wait(last.at[peer(back(dy), flip)[1]], fsem.at[i])
            for h in range(HALVES):
                res[0, :, h * W:(h + 1) * W] = last[pl.ds(h * NY, NY)].reshape(W, CL).T
            pltpu.make_async_copy(res, out, osem).start()

    def loads():
        pltpu.make_async_copy(incident, inc, lsem.at[3]).start()
        pltpu.make_async_copy(tiles, tl.at[row], lsem.at[4]).start()
        for i, dy in enumerate((1, 3, 2)):
            send(tiles, tl.at[row], tsend, tsem.at[i], peer(back(dy), 0)[0], col)
        send(tiles, tl.at[row], tsend, tsem.at[3], y * 2 + other, col)
        for a, rel in order:
            gx = lax.rem(x + rel, NX)
            for l in range(LH):
                pltpu.make_async_copy(
                    kernels.at[a * LH + l, :, pl.ds(pl.multiple_of(gx * (NZ * SRC), 128), NZ * SRC)],
                    kb.at[a * NX + rel, :, pl.ds(l * NZ * SRC, NZ * SRC)],
                    ksem.at[a * NX + rel, l],
                ).start()

    events.append((0.02, 1000, loads))

    gather(0, 0.0, 3.2)
    gather(1, 0.01, 3.2)
    exchange(15.0)
    summed(30.0, 31.4, 38.0)
    for s in range(SWEEPS):
        sweep(s, 40.0 + 7 * s, 46.0 + 7 * s)
    finish(65.0)

    for _, _, f in sorted(events, key=lambda e: e[:2]):
        f()

    wait(tl.at[pl.ds(0, 7)], tsend)
    wait(icd.at[pl.ds(0, 7)], isend)
    for i in range(7):
        wait(codes.at[0], csend.at[i])
    for h in range(HALVES):
        for d in range(2):
            wait(hb.at[h, :, pl.ds(0, 3), :, pl.ds(0, 240), :], gsend.at[h, d])
    wait(sp, psend)
    wait(ts.at[pl.ds(0, 6)], ysend)
    for s in range(SWEEPS):
        wait(gat[s].at[pl.ds(0, 2)], ssend.at[s])
    wait(fin.at[pl.ds(0, 7)], fsend)
    wait(res, osem)


def per_device(kernels, history, incident, owner, pairs, tiles, counts):
    dma = pltpu.SemaphoreType.DMA
    any_ = pl.BlockSpec(memory_space=pl.ANY)
    return pl.pallas_call(
        body,
        out_shape=jax.ShapeDtypeStruct(incident.shape, F32),
        in_specs=[any_] * 7,
        out_specs=any_,
        scratch_shapes=[
            pltpu.VMEM((HALVES, 2, NX, LH, NZ * SRC, W), BF16),
            pltpu.VMEM((2 * NX, 8 * CL, DEPTH), BF16),
            pltpu.VMEM((HALVES, 8, CL, W), F32),
            *[pltpu.VMEM((8, W, CL), F32)] * 4,
            pltpu.VMEM((3, 8, CW, CL), F32),
            pltpu.VMEM((1, CL, COLS), F32),
            *[pltpu.VMEM((8, CW, CL), F32)] * 6,
            pltpu.VMEM((1, CL, COLS), F32),
            pltpu.VMEM((8, TILES, CL, CL), BF16),
            *[pltpu.VMEM((3, 8, CW, CL), BF16)] * SWEEPS,
            pltpu.SMEM((128,), jnp.int32),
            pltpu.SMEM((2, TILES), jnp.int32),
            pltpu.SMEM((1,), jnp.int32),
            pltpu.SMEM((8, 16), jnp.int32),
            dma((5,)), dma((8, LH)), dma((HALVES, 2)), dma((HALVES, 2, 5, 4)), dma((HALVES, 2)),
            dma((7,)), dma, dma((7,)), dma, dma((7,)), dma((7,)),
            dma((8,)), dma, dma((3, 2)), dma, dma((SWEEPS, 2)), dma((SWEEPS,)), dma((7,)), dma, dma,
        ],
        compiler_params=pltpu.CompilerParams(
            collective_id=0, has_side_effects=True, vmem_limit_bytes=56 * 2**20
        ),
        cost_estimate=pl.CostEstimate(flops=5_200_000_000, bytes_accessed=21_000_000, transcendentals=0),
    )(kernels, history, incident, owner, pairs.T, tiles, counts)


def solution(mesh):
    both = ("row", "col")
    in_specs = (
        P(None, "col", "row"), P(None, both, None), P(both, None, None), P(),
        P(both, None), P(both, None, None), P(both),
    )
    return jax.shard_map(
        per_device, mesh=mesh, in_specs=in_specs, out_specs=P(both, None, None), check_vma=False
    )
```

```python
import functools

import jax
import jax.numpy as jnp
from jax import lax
from jax.experimental import pallas as pl
from jax.experimental.pallas import tpu as pltpu
from jax.sharding import PartitionSpec as P

MESH = pl.DeviceIdType.MESH
F32, BF16 = jnp.float32, jnp.bfloat16

SWEEPS = 3
DAMPING = 0.7

NX, NZ, NY = 4, 4, 4
LAGS, SRC, COLS, CL = 6, 96, 256, 128
HALVES = 2
W = COLS // HALVES
CW = COLS // 8
LH = LAGS // 2
DEPTH = LH * NZ * SRC
TILES = 12


def body(kernels, history, incident, owner, pairs, tiles, counts, out,
         hb, kb, acc, mine, sp, rp, ts, ry, inc, ict, icd, drv, den, fin, last, res, tin, tl,
         gat0, gat1, gat2, owner_s, pairs_s, counts_s, codes,
         lsem, ksem, hsem, gsem, gsend, tsem, tsend, isem, isend, csem, csend,
         psem, psend, ysem, ysend, ssem, ssend, fsem, fsend, osem):
    row, col = lax.axis_index("row"), lax.axis_index("col")
    y, core = lax.div(row, 2), lax.rem(row, 2)
    x, z = lax.div(col, NZ), lax.rem(col, NZ)
    other = 1 - core

    def at_col(dx, dz):
        return lax.rem(x + dx + NX, NX) * NZ + lax.rem(z + dz + NZ, NZ)

    def at_row(dy):
        return lax.rem(y + dy + NY, NY) * 2 + core

    def near_col(dc):
        return lax.rem(col + dc + NX * NZ, NX * NZ)

    def send(src, dst, ssem_, rsem_, r, c):
        pltpu.make_async_remote_copy(
            src_ref=src, dst_ref=dst, send_sem=ssem_, recv_sem=rsem_,
            device_id={"row": r, "col": c}, device_id_type=MESH,
        ).start()

    def wait(ref, sem):
        pltpu.make_async_copy(ref, ref, sem).wait()

    gat = (gat0, gat1, gat2)

    barrier = pltpu.get_barrier_semaphore()
    greet = [(row, at_col(1, 0)), (row, at_col(-1, 0)), (row, at_col(0, 1)), (row, at_col(0, -1))]
    greet += [(at_row(1), col), (at_row(-1), col), (at_row(2), col), (y * 2 + other, col)]
    greet += [(at_row(dy) + other - core, col) for dy in (1, 2, 3)]
    for r, c in greet:
        pl.semaphore_signal(barrier, inc=1, device_id={"row": r, "col": c}, device_id_type=MESH)

    def piece(h, a, dx, dz, lo=0, n=SRC):
        zr = pl.multiple_of(lax.rem(z + dz + NZ, NZ) * SRC + lo, 16)
        return hb.at[h, a, dx % NX, :, pl.ds(zr, n), :]

    def own(h, a):
        return history.at[pl.ds(a * LH, LH), :, pl.ds(h * W, W)]

    for h in range(HALVES):
        for a in range(2):
            pltpu.make_async_copy(own(h, a), piece(h, a, 0, 0), hsem.at[h, a]).start()
    pltpu.make_async_copy(owner, owner_s, lsem.at[0]).start()
    pltpu.make_async_copy(pairs, pairs_s, lsem.at[1]).start()
    pltpu.make_async_copy(counts, counts_s, lsem.at[2]).start()
    pl.semaphore_wait(barrier, len(greet))

    events = []

    def at(t):
        def add(f):
            events.append((t, len(events), f))
        return add

    def axis(a, phase):
        return ((1, 0), (0, 1))[(a + phase) % 2]

    def move(h, a, off, d, lo, n, sem, first=False):
        src = own(h, a) if first else piece(h, a, off[0], off[1], lo, n)
        zr = pl.multiple_of(lax.rem(z + off[1] + NZ, NZ) * SRC + lo, 16)
        dst = hb.at[h, a, (off[0] - d[0]) % NX, :, pl.ds(zr, n), :]
        send(src, dst, gsend.at[h, 0 if d[0] else 1], sem, row, at_col(d[0], d[1]))

    def neg(d):
        return (-d[0], -d[1])

    def mul(d, k):
        return (d[0] * k, d[1] * k)

    def add2(p, q):
        return (p[0] + q[0], p[1] + q[1])

    half = SRC // 2

    def spread(h, a, off, j, first=False):
        d = axis(a, 1)
        move(h, a, off, d, 0, SRC, gsem.at[h, a, j, 0], first)
        move(h, a, off, neg(d), 0, SRC, gsem.at[h, a, j, 1], first)

    def relay(h, a, off, j, d):
        lo, hi = add2(off, neg(d)), add2(off, d)
        wait(piece(h, a, *lo), gsem.at[h, a, j, 0])
        move(h, a, lo, d, 0, half, gsem.at[h, a, j, 2])
        wait(piece(h, a, *hi), gsem.at[h, a, j, 1])
        move(h, a, hi, neg(d), half, half, gsem.at[h, a, j, 3])

    def far(h, a, off, j, d):
        o = add2(off, mul(d, 2))
        wait(piece(h, a, o[0], o[1], 0, half), gsem.at[h, a, j, 2])
        wait(piece(h, a, o[0], o[1], half, half), gsem.at[h, a, j, 3])

    order = [(1, 0), (0, 0), (1, 3), (1, 1), (0, 3), (0, 1), (1, 2), (0, 2)]

    def mm(a, dx):
        g = a * NX + dx % NX
        for l in range(LH):
            wait(kb.at[g, :, pl.ds(l * NZ * SRC, NZ * SRC)], ksem.at[g, l])
        w = jnp.concatenate([hb[h, a, dx % NX].reshape(DEPTH, W) for h in range(HALVES)], axis=1)
        d = jnp.dot(kb[g], w, preferred_element_type=F32)
        for h in range(HALVES):
            part = d[:, h * W:(h + 1) * W].reshape(2 * NY, CL, W)
            acc[h] = part if (a, dx % NX) == order[0] else acc[h] + part

    def product(h, t0, a, dx):
        if h == HALVES - 1:
            @at(t0)
            def _():
                mm(a, dx)

    def gather(h, t0, u):
        @at(t0)
        def _():
            for a in range(2):
                d = axis(a, 0)
                move(h, a, (0, 0), d, 0, SRC, gsem.at[h, a, 0, 0], True)
                move(h, a, (0, 0), neg(d), 0, SRC, gsem.at[h, a, 0, 1], True)
            for a in range(2):
                spread(h, a, (0, 0), 1, True)

        @at(t0 + 1.2 * u)
        def _():
            for a in range(2):
                p = axis(a, 0)
                relay(h, a, (0, 0), 0, p)
            for a in range(2):
                p = axis(a, 0)
                spread(h, a, neg(p), 2)
                spread(h, a, p, 3)

        @at(t0 + 2.2 * u)
        def _():
            for a in range(2):
                relay(h, a, (0, 0), 1, axis(a, 1))

        @at(t0 + 2.7 * u)
        def _():
            for a in range(2):
                p = axis(a, 0)
                far(h, a, (0, 0), 0, p)
                spread(h, a, mul(p, 2), 4)
            for a in range(2):
                wait(piece(h, a, 0, 0), hsem.at[h, a])

        product(h, t0 + 2.7 * u, 1, 0)

        @at(t0 + 3.7 * u)
        def _():
            for a in range(2):
                relay(h, a, neg(axis(a, 0)), 2, axis(a, 1))

        @at(t0 + 4.7 * u)
        def _():
            for a in range(2):
                relay(h, a, axis(a, 0), 3, axis(a, 1))

        @at(t0 + 5.2 * u)
        def _():
            for a in range(2):
                far(h, a, (0, 0), 1, axis(a, 1))

        product(h, t0 + 5.2 * u, 0, 0)

        @at(t0 + 6.2 * u)
        def _():
            for a in range(2):
                relay(h, a, mul(axis(a, 0), 2), 4, axis(a, 1))

        product(h, t0 + 6.3 * u, 1, -1)

        product(h, t0 + 6.5 * u, 1, 1)

        @at(t0 + 6.8 * u)
        def _():
            for a in range(2):
                far(h, a, neg(axis(a, 0)), 2, axis(a, 1))

        product(h, t0 + 6.8 * u, 0, -1)

        @at(t0 + 7.3 * u)
        def _():
            for a in range(2):
                far(h, a, axis(a, 0), 3, axis(a, 1))

        product(h, t0 + 7.3 * u, 0, 1)

        @at(t0 + 7.8 * u)
        def _():
            far(h, 1, mul(axis(1, 0), 2), 4, axis(1, 1))

        product(h, t0 + 7.8 * u, 1, 2)

        @at(t0 + 7.8 * u)
        def _():
            far(h, 0, mul(axis(0, 0), 2), 4, axis(0, 1))

        product(h, t0 + 7.8 * u, 0, 2)

    part = core * NY + y
    peers = [(dy, flip) for dy in (2, 1, 3) for flip in (0, 1)] + [(0, 1)]

    def peer(dy, flip):
        y2 = lax.rem(y + dy, NY)
        k2 = other if flip else core
        return y2 * 2 + k2, k2 * NY + y2

    def position(r):
        p = jnp.int32(0)
        for b in range(NY * 2):
            p = p + jnp.where(owner_s[col * (NY * 2) + b] == r, b, 0)
        return jnp.minimum(p, NY * 2 - 1)

    tab = {}

    @at(1.0)
    def _():
        wait(tin, lsem.at[4])
        for t in range(TILES):
            tl[row, t] = tin[t].T
        for i, dy in enumerate((1, 3, 2)):
            send(tl.at[row], tl.at[row], tsend, tsem.at[i], peer(back(dy), 0)[0], col)
        send(tl.at[row], tl.at[row], tsend, tsem.at[3], y * 2 + other, col)

    @at(2.0)
    def _():
        wait(owner_s, lsem.at[0])
        wait(pairs_s, lsem.at[1])
        wait(counts_s, lsem.at[2])
        for t in range(TILES):
            s = jnp.clip(pairs_s[1, t], 0, CL - 1)
            zi = jnp.minimum(lax.rem(lax.shift_right_logical(s, 3) - col + 2 * NX * NZ + 1, NX * NZ), 2)
            codes[row, t] = jnp.where(t < counts_s[0], zi * (2 * NY) + owner_s[s], -1)
        for t in range(TILES, 16):
            codes[row, t] = -1
        wait(inc, lsem.at[3])
        for h in range(HALVES):
            ict[pl.ds(h * NY, NY)] = inc[0, :, h * W:(h + 1) * W].T.reshape(NY, CW, CL)
        icd[row] = ict[part]
        for i, (dy, flip) in enumerate(peers):
            r, p = peer(dy, flip)
            send(ict.at[p], icd.at[row], isend, isem.at[i], r, col)
            send(codes.at[row], codes.at[row], csend.at[i], csem.at[i], r, col)

    def exchange(t0):
        @at(t0)
        def _():
            for i, dy in enumerate((1, 3, 2)):
                r = peer(dy, 0)[0]
                wait(tl.at[r], tsem.at[i])
                send(tl.at[r], tl.at[r], tsend, tsem.at[4 + i], y * 2 + other, col)

    def back(dy):
        return (NY - dy) % NY

    def summed(t0, t1, t2):
        @at(t0)
        def _():
            pos = [position(jnp.int32(r)) for r in range(2 * NY)]
            for r in range(2 * NY):
                sp[r] = acc[other, pos[r]].T
                send(sp.at[r], rp.at[r], psend, psem.at[r], y * 2 + other, col)
            for r in range(2 * NY):
                mine[r] = acc[core, pos[r]].T

        @at(t1)
        def _():
            for g in range(2):
                for r in range(g * NY, g * NY + NY):
                    wait(rp.at[r], psem.at[r])
                    ts[r] = mine[r] + rp[r]
                for i, dy in enumerate((2, 1, 3)):
                    y2 = lax.rem(y + dy, NY)
                    send(ts.at[pl.ds(g * NY, NY), pl.ds(pl.multiple_of(y2 * CW, CW), CW)],
                         ry.at[i, pl.ds(g * NY, NY)], ysend, ysem.at[i, g], y2 * 2 + core, col)
            for i in range(7):
                dy, flip = peers[i]
                wait(icd.at[peer(back(dy), flip)[0]], isem.at[i])
            drv[...] = icd[...] - ts[:, pl.ds(pl.multiple_of(y * CW, CW), CW)]

        @at(t2)
        def _():
            for g in range(2):
                rows = pl.ds(g * NY, NY)
                for i in (1, 2, 0):
                    wait(ry.at[i, rows], ysem.at[i, g])
                drv[rows] = drv[rows] - (ry[0, rows] + (ry[1, rows] + ry[2, rows]))
                gat[0][1, rows] = drv[rows].astype(BF16)
                halo(0, g)

    def halo(s, g):
        src = gat[s].at[1, pl.ds(g * NY, NY)]
        for i, (dc, zi) in enumerate(((1, 0), (-1, 2))):
            send(src, gat[s].at[zi, pl.ds(g * NY, NY)], ssend.at[s], ssem.at[s, i, g], row, near_col(dc))

    def sweep(s, t1):
        g = gat[s]

        def one(r):
            blocks = []
            for t in range(TILES):
                c = codes[r, t]
                i = jnp.clip(c, 0, 6 * NY - 1)
                u = g[lax.shift_right_logical(i, 3), lax.rem(i, 2 * NY)]
                blocks.append(jnp.where(c >= 0, u, jnp.zeros((), BF16)))
            near = jnp.dot(jnp.concatenate(blocks, axis=1), tl[r].reshape(TILES * CL, CL), preferred_element_type=F32)
            d = drv[r]
            cur = d if s == 0 else den[r]
            return cur + DAMPING * (d - cur - near)

        @at(t1)
        def _():
            if s == 0:
                for i, (dy, flip) in enumerate(peers):
                    wait(codes.at[peer(back(dy), flip)[0]], csem.at[i])
                for i, dy in enumerate((1, 3, 2)):
                    wait(tl.at[peer(dy, 1)[0]], tsem.at[4 + i])
                wait(tl.at[peer(0, 1)[0]], tsem.at[3])
            for k in range(2):
                for i, zi in enumerate((0, 2)):
                    wait(g.at[zi, pl.ds(k * NY, NY)], ssem.at[s, i, k])
            if s < SWEEPS - 1:
                for r in range(2 * NY):
                    new = one(r)
                    den[r] = new
                    gat[s + 1][1, r] = new.astype(BF16)
                    if r % NY == NY - 1:
                        halo(s + 1, r // NY)
            else:
                for i, (dy, flip) in enumerate(peers):
                    r = peer(dy, flip)[0]
                    fin[r] = one(r)
                    send(fin.at[r], last.at[part], fsend, fsem.at[i], r, col)
                last[part] = one(row)

    def finish(t0):
        @at(t0)
        def _():
            for i, (dy, flip) in enumerate(peers):
                wait(last.at[peer(back(dy), flip)[1]], fsem.at[i])
            for h in range(HALVES):
                res[0, :, h * W:(h + 1) * W] = last[pl.ds(h * NY, NY)].reshape(W, CL).T
            pltpu.make_async_copy(res, out, osem).start()

    def loads():
        pltpu.make_async_copy(incident, inc, lsem.at[3]).start()
        pltpu.make_async_copy(tiles, tin, lsem.at[4]).start()
        for a, rel in order:
            gx = lax.rem(x + rel, NX)
            for l in range(LH):
                pltpu.make_async_copy(
                    kernels.at[a * LH + l, :, pl.ds(pl.multiple_of(gx * (NZ * SRC), 128), NZ * SRC)],
                    kb.at[a * NX + rel, :, pl.ds(l * NZ * SRC, NZ * SRC)],
                    ksem.at[a * NX + rel, l],
                ).start()

    events.append((0.02, 1000, loads))

    gather(0, 0.0, 3.2)
    gather(1, 0.01, 3.2)
    exchange(24.9)
    summed(30.0, 31.4, 38.0)
    for s in range(SWEEPS):
        sweep(s, 46.0 + 7 * s)
    finish(65.0)

    for _, _, f in sorted(events, key=lambda e: e[:2]):
        f()

    wait(tl.at[pl.ds(0, 7)], tsend)
    wait(icd.at[pl.ds(0, 7)], isend)
    for i in range(7):
        wait(codes.at[0], csend.at[i])
    for h in range(HALVES):
        for d in range(2):
            wait(hb.at[h, :, pl.ds(0, 3), :, pl.ds(0, 240), :], gsend.at[h, d])
    wait(sp, psend)
    wait(ts.at[pl.ds(0, 6)], ysend)
    for s in range(SWEEPS):
        wait(gat[s].at[pl.ds(0, 2)], ssend.at[s])
    wait(fin.at[pl.ds(0, 7)], fsend)
    wait(res, osem)


def per_device(kernels, history, incident, owner, pairs, tiles, counts):
    dma = pltpu.SemaphoreType.DMA
    any_ = pl.BlockSpec(memory_space=pl.ANY)
    return pl.pallas_call(
        body,
        out_shape=jax.ShapeDtypeStruct(incident.shape, F32),
        in_specs=[any_] * 7,
        out_specs=any_,
        scratch_shapes=[
            pltpu.VMEM((HALVES, 2, NX, LH, NZ * SRC, W), BF16),
            pltpu.VMEM((2 * NX, 8 * CL, DEPTH), BF16),
            pltpu.VMEM((HALVES, 8, CL, W), F32),
            *[pltpu.VMEM((8, W, CL), F32)] * 4,
            pltpu.VMEM((3, 8, CW, CL), F32),
            pltpu.VMEM((1, CL, COLS), F32),
            *[pltpu.VMEM((8, CW, CL), F32)] * 6,
            pltpu.VMEM((1, CL, COLS), F32),
            pltpu.VMEM((TILES, CL, CL), BF16),
            pltpu.VMEM((8, TILES, CL, CL), BF16),
            *[pltpu.VMEM((3, 8, CW, CL), BF16)] * SWEEPS,
            pltpu.SMEM((128,), jnp.int32),
            pltpu.SMEM((2, TILES), jnp.int32),
            pltpu.SMEM((1,), jnp.int32),
            pltpu.SMEM((8, 16), jnp.int32),
            dma((5,)), dma((8, LH)), dma((HALVES, 2)), dma((HALVES, 2, 5, 4)), dma((HALVES, 2)),
            dma((7,)), dma, dma((7,)), dma, dma((7,)), dma((7,)),
            dma((8,)), dma, dma((3, 2)), dma, dma((SWEEPS, 2, 2)), dma((SWEEPS,)), dma((7,)), dma, dma,
        ],
        compiler_params=pltpu.CompilerParams(
            collective_id=0, has_side_effects=True, vmem_limit_bytes=56 * 2**20
        ),
        cost_estimate=pl.CostEstimate(flops=5_200_000_000, bytes_accessed=21_000_000, transcendentals=0),
    )(kernels, history, incident, owner, pairs.T, tiles, counts)


def solution(mesh):
    both = ("row", "col")
    in_specs = (
        P(None, "col", "row"), P(None, both, None), P(both, None, None), P(),
        P(both, None), P(both, None, None), P(both),
    )
    return jax.shard_map(
        per_device, mesh=mesh, in_specs=in_specs, out_specs=P(both, None, None), check_vma=False
    )
```

```python
import functools

import jax
import jax.numpy as jnp
from jax import lax
from jax.experimental import pallas as pl
from jax.experimental.pallas import tpu as pltpu
from jax.sharding import PartitionSpec as P

MESH = pl.DeviceIdType.MESH
F32, BF16 = jnp.float32, jnp.bfloat16

SWEEPS = 3
DAMPING = 0.7

NX, NZ, NY = 4, 4, 4
LAGS, SRC, COLS, CL = 6, 96, 256, 128
HALVES = 2
W = COLS // HALVES
CW = COLS // 8
LH = LAGS // 2
DEPTH = LH * NZ * SRC
TILES = 12


def body(kernels, history, incident, owner, pairs, tiles, counts, out,
         hb, kb, acc, mine, sp, rp, ts, ry, inc, ict, icd, drv, den, fin, last, res, tin, tl,
         gat0, gat1, gat2, owner_s, pairs_s, counts_s, codes,
         lsem, ksem, hsem, gsem, gsend, tsem, tsend, isem, isend, csem, csend,
         psem, psend, ysem, ysend, ssem, ssend, fsem, fsend, osem):
    row, col = lax.axis_index("row"), lax.axis_index("col")
    y, core = lax.div(row, 2), lax.rem(row, 2)
    x, z = lax.div(col, NZ), lax.rem(col, NZ)
    other = 1 - core

    def at_col(dx, dz):
        return lax.rem(x + dx + NX, NX) * NZ + lax.rem(z + dz + NZ, NZ)

    def at_row(dy):
        return lax.rem(y + dy + NY, NY) * 2 + core

    def near_col(dc):
        return lax.rem(col + dc + NX * NZ, NX * NZ)

    def send(src, dst, ssem_, rsem_, r, c):
        pltpu.make_async_remote_copy(
            src_ref=src, dst_ref=dst, send_sem=ssem_, recv_sem=rsem_,
            device_id={"row": r, "col": c}, device_id_type=MESH,
        ).start()

    def wait(ref, sem):
        pltpu.make_async_copy(ref, ref, sem).wait()

    gat = (gat0, gat1, gat2)

    barrier = pltpu.get_barrier_semaphore()
    greet = [(row, at_col(1, 0)), (row, at_col(-1, 0)), (row, at_col(0, 1)), (row, at_col(0, -1))]
    greet += [(at_row(1), col), (at_row(-1), col), (at_row(2), col), (y * 2 + other, col)]
    greet += [(at_row(dy) + other - core, col) for dy in (1, 2, 3)]
    for r, c in greet:
        pl.semaphore_signal(barrier, inc=1, device_id={"row": r, "col": c}, device_id_type=MESH)

    def piece(h, a, dx, dz, lo=0, n=SRC):
        zr = pl.multiple_of(lax.rem(z + dz + NZ, NZ) * SRC + lo, 16)
        return hb.at[h, a, dx % NX, :, pl.ds(zr, n), :]

    def own(h, a):
        return history.at[pl.ds(a * LH, LH), :, pl.ds(h * W, W)]

    for h in range(HALVES):
        for a in range(2):
            pltpu.make_async_copy(own(h, a), piece(h, a, 0, 0), hsem.at[h, a]).start()
    pltpu.make_async_copy(tiles, tin, lsem.at[4]).start()
    pltpu.make_async_copy(owner, owner_s, lsem.at[0]).start()
    pltpu.make_async_copy(pairs, pairs_s, lsem.at[1]).start()
    pltpu.make_async_copy(counts, counts_s, lsem.at[2]).start()
    pl.semaphore_wait(barrier, len(greet))

    events = []

    def at(t):
        def add(f):
            events.append((t, len(events), f))
        return add

    def axis(a, phase):
        return ((1, 0), (0, 1))[(a + phase) % 2]

    def move(h, a, off, d, lo, n, sem, first=False):
        src = own(h, a) if first else piece(h, a, off[0], off[1], lo, n)
        zr = pl.multiple_of(lax.rem(z + off[1] + NZ, NZ) * SRC + lo, 16)
        dst = hb.at[h, a, (off[0] - d[0]) % NX, :, pl.ds(zr, n), :]
        send(src, dst, gsend.at[h, 0 if d[0] else 1], sem, row, at_col(d[0], d[1]))

    def neg(d):
        return (-d[0], -d[1])

    def mul(d, k):
        return (d[0] * k, d[1] * k)

    def add2(p, q):
        return (p[0] + q[0], p[1] + q[1])

    half = SRC // 2

    def spread(h, a, off, j, first=False):
        d = axis(a, 1)
        move(h, a, off, d, 0, SRC, gsem.at[h, a, j, 0], first)
        move(h, a, off, neg(d), 0, SRC, gsem.at[h, a, j, 1], first)

    def relay(h, a, off, j, d):
        lo, hi = add2(off, neg(d)), add2(off, d)
        wait(piece(h, a, *lo), gsem.at[h, a, j, 0])
        move(h, a, lo, d, 0, half, gsem.at[h, a, j, 2])
        wait(piece(h, a, *hi), gsem.at[h, a, j, 1])
        move(h, a, hi, neg(d), half, half, gsem.at[h, a, j, 3])

    def far(h, a, off, j, d):
        o = add2(off, mul(d, 2))
        wait(piece(h, a, o[0], o[1], 0, half), gsem.at[h, a, j, 2])
        wait(piece(h, a, o[0], o[1], half, half), gsem.at[h, a, j, 3])

    order = [(1, 0), (0, 0), (1, 3), (1, 1), (0, 3), (0, 1), (1, 2), (0, 2)]

    def mm(a, dx):
        g = a * NX + dx % NX
        for l in range(LH):
            wait(kb.at[g, :, pl.ds(l * NZ * SRC, NZ * SRC)], ksem.at[g, l])
        w = jnp.concatenate([hb[h, a, dx % NX].reshape(DEPTH, W) for h in range(HALVES)], axis=1)
        d = jnp.dot(kb[g], w, preferred_element_type=F32)
        for h in range(HALVES):
            part = d[:, h * W:(h + 1) * W].reshape(2 * NY, CL, W)
            acc[h] = part if (a, dx % NX) == order[0] else acc[h] + part

    def product(h, t0, a, dx):
        if h == HALVES - 1:
            @at(t0)
            def _():
                mm(a, dx)

    def gather(h, t0, u):
        @at(t0)
        def _():
            for a in range(2):
                d = axis(a, 0)
                move(h, a, (0, 0), d, 0, SRC, gsem.at[h, a, 0, 0], True)
                move(h, a, (0, 0), neg(d), 0, SRC, gsem.at[h, a, 0, 1], True)
            for a in range(2):
                spread(h, a, (0, 0), 1, True)

        @at(t0 + 1.2 * u)
        def _():
            for a in range(2):
                p = axis(a, 0)
                relay(h, a, (0, 0), 0, p)
            for a in range(2):
                p = axis(a, 0)
                spread(h, a, neg(p), 2)
                spread(h, a, p, 3)

        @at(t0 + 2.2 * u)
        def _():
            for a in range(2):
                relay(h, a, (0, 0), 1, axis(a, 1))

        @at(t0 + 2.7 * u)
        def _():
            for a in range(2):
                p = axis(a, 0)
                far(h, a, (0, 0), 0, p)
                spread(h, a, mul(p, 2), 4)
            for a in range(2):
                wait(piece(h, a, 0, 0), hsem.at[h, a])

        product(h, t0 + 2.7 * u, 1, 0)

        @at(t0 + 3.7 * u)
        def _():
            for a in range(2):
                relay(h, a, neg(axis(a, 0)), 2, axis(a, 1))

        @at(t0 + 4.7 * u)
        def _():
            for a in range(2):
                relay(h, a, axis(a, 0), 3, axis(a, 1))

        @at(t0 + 5.2 * u)
        def _():
            for a in range(2):
                far(h, a, (0, 0), 1, axis(a, 1))

        product(h, t0 + 5.2 * u, 0, 0)

        @at(t0 + 6.2 * u)
        def _():
            for a in range(2):
                relay(h, a, mul(axis(a, 0), 2), 4, axis(a, 1))

        product(h, t0 + 6.3 * u, 1, -1)

        product(h, t0 + 6.5 * u, 1, 1)

        @at(t0 + 6.8 * u)
        def _():
            for a in range(2):
                far(h, a, neg(axis(a, 0)), 2, axis(a, 1))

        product(h, t0 + 6.8 * u, 0, -1)

        @at(t0 + 7.3 * u)
        def _():
            for a in range(2):
                far(h, a, axis(a, 0), 3, axis(a, 1))

        product(h, t0 + 7.3 * u, 0, 1)

        @at(t0 + 7.8 * u)
        def _():
            far(h, 1, mul(axis(1, 0), 2), 4, axis(1, 1))

        product(h, t0 + 7.8 * u, 1, 2)

        @at(t0 + 7.8 * u)
        def _():
            far(h, 0, mul(axis(0, 0), 2), 4, axis(0, 1))

        product(h, t0 + 7.8 * u, 0, 2)

    part = core * NY + y
    peers = [(dy, flip) for dy in (2, 1, 3) for flip in (0, 1)] + [(0, 1)]

    def peer(dy, flip):
        y2 = lax.rem(y + dy, NY)
        k2 = other if flip else core
        return y2 * 2 + k2, k2 * NY + y2

    def position(r):
        p = jnp.int32(0)
        for b in range(NY * 2):
            p = p + jnp.where(owner_s[col * (NY * 2) + b] == r, b, 0)
        return jnp.minimum(p, NY * 2 - 1)

    tab = {}

    @at(0.015)
    def _():
        wait(tin, lsem.at[4])
        for t in range(TILES):
            tl[row, t] = tin[t].T
        for i, dy in enumerate((1, 3, 2)):
            send(tl.at[row], tl.at[row], tsend, tsem.at[i], peer(back(dy), 0)[0], col)
        send(tl.at[row], tl.at[row], tsend, tsem.at[3], y * 2 + other, col)

    @at(2.0)
    def _():
        wait(owner_s, lsem.at[0])
        wait(pairs_s, lsem.at[1])
        wait(counts_s, lsem.at[2])
        for t in range(TILES):
            s = jnp.clip(pairs_s[1, t], 0, CL - 1)
            zi = jnp.minimum(lax.rem(lax.shift_right_logical(s, 3) - col + 2 * NX * NZ + 1, NX * NZ), 2)
            codes[row, t] = jnp.where(t < counts_s[0], zi * (2 * NY) + owner_s[s], -1)
        for t in range(TILES, 16):
            codes[row, t] = -1
        wait(inc, lsem.at[3])
        for h in range(HALVES):
            ict[pl.ds(h * NY, NY)] = inc[0, :, h * W:(h + 1) * W].T.reshape(NY, CW, CL)
        icd[row] = ict[part]
        for i, (dy, flip) in enumerate(peers):
            r, p = peer(dy, flip)
            send(ict.at[p], icd.at[row], isend, isem.at[i], r, col)
            send(codes.at[row], codes.at[row], csend.at[i], csem.at[i], r, col)

    def exchange(t0):
        @at(t0)
        def _():
            for i, dy in enumerate((1, 3, 2)):
                r = peer(dy, 0)[0]
                wait(tl.at[r], tsem.at[i])
                send(tl.at[r], tl.at[r], tsend, tsem.at[4 + i], y * 2 + other, col)

    def back(dy):
        return (NY - dy) % NY

    def summed(t0, t1, t2):
        @at(t0)
        def _():
            pos = [position(jnp.int32(r)) for r in range(2 * NY)]
            for r in range(2 * NY):
                sp[r] = acc[other, pos[r]].T
                send(sp.at[r], rp.at[r], psend, psem.at[r], y * 2 + other, col)
            for r in range(2 * NY):
                mine[r] = acc[core, pos[r]].T

        @at(t1)
        def _():
            for g in range(2):
                for r in range(g * NY, g * NY + NY):
                    wait(rp.at[r], psem.at[r])
                    ts[r] = mine[r] + rp[r]
                for i, dy in enumerate((2, 1, 3)):
                    y2 = lax.rem(y + dy, NY)
                    send(ts.at[pl.ds(g * NY, NY), pl.ds(pl.multiple_of(y2 * CW, CW), CW)],
                         ry.at[i, pl.ds(g * NY, NY)], ysend, ysem.at[i, g], y2 * 2 + core, col)
            for i in range(7):
                dy, flip = peers[i]
                wait(icd.at[peer(back(dy), flip)[0]], isem.at[i])
            drv[...] = icd[...] - ts[:, pl.ds(pl.multiple_of(y * CW, CW), CW)]

        @at(t2)
        def _():
            for g in range(2):
                rows = pl.ds(g * NY, NY)
                for i in (1, 2, 0):
                    wait(ry.at[i, rows], ysem.at[i, g])
                drv[rows] = drv[rows] - (ry[0, rows] + (ry[1, rows] + ry[2, rows]))
                gat[0][1, rows] = drv[rows].astype(BF16)
                halo(0, g)

    def halo(s, g):
        src = gat[s].at[1, pl.ds(g * NY, NY)]
        for i, (dc, zi) in enumerate(((1, 0), (-1, 2))):
            send(src, gat[s].at[zi, pl.ds(g * NY, NY)], ssend.at[s], ssem.at[s, i, g], row, near_col(dc))

    def sweep(s, t1):
        g = gat[s]

        def one(r):
            blocks = []
            for t in range(TILES):
                c = codes[r, t]
                i = jnp.clip(c, 0, 6 * NY - 1)
                u = g[lax.shift_right_logical(i, 3), lax.rem(i, 2 * NY)]
                blocks.append(jnp.where(c >= 0, u, jnp.zeros((), BF16)))
            near = jnp.dot(jnp.concatenate(blocks, axis=1), tl[r].reshape(TILES * CL, CL), preferred_element_type=F32)
            d = drv[r]
            cur = d if s == 0 else den[r]
            return cur + DAMPING * (d - cur - near)

        @at(t1)
        def _():
            if s == 0:
                for i, (dy, flip) in enumerate(peers):
                    wait(codes.at[peer(back(dy), flip)[0]], csem.at[i])
                for i, dy in enumerate((1, 3, 2)):
                    wait(tl.at[peer(dy, 1)[0]], tsem.at[4 + i])
                wait(tl.at[peer(0, 1)[0]], tsem.at[3])
            for k in range(2):
                for i, zi in enumerate((0, 2)):
                    wait(g.at[zi, pl.ds(k * NY, NY)], ssem.at[s, i, k])
            if s < SWEEPS - 1:
                for r in range(2 * NY):
                    new = one(r)
                    den[r] = new
                    gat[s + 1][1, r] = new.astype(BF16)
                    if r % NY == NY - 1:
                        halo(s + 1, r // NY)
            else:
                for i, (dy, flip) in enumerate(peers):
                    r = peer(dy, flip)[0]
                    fin[r] = one(r)
                    send(fin.at[r], last.at[part], fsend, fsem.at[i], r, col)
                last[part] = one(row)

    def finish(t0):
        @at(t0)
        def _():
            for i, (dy, flip) in enumerate(peers):
                wait(last.at[peer(back(dy), flip)[1]], fsem.at[i])
            for h in range(HALVES):
                res[0, :, h * W:(h + 1) * W] = last[pl.ds(h * NY, NY)].reshape(W, CL).T
            pltpu.make_async_copy(res, out, osem).start()

    def loads():
        pltpu.make_async_copy(incident, inc, lsem.at[3]).start()
        for a, rel in order:
            gx = lax.rem(x + rel, NX)
            for l in range(LH):
                pltpu.make_async_copy(
                    kernels.at[a * LH + l, :, pl.ds(pl.multiple_of(gx * (NZ * SRC), 128), NZ * SRC)],
                    kb.at[a * NX + rel, :, pl.ds(l * NZ * SRC, NZ * SRC)],
                    ksem.at[a * NX + rel, l],
                ).start()

    events.append((0.02, 1000, loads))

    gather(0, 0.0, 3.2)
    gather(1, 0.01, 3.2)
    exchange(24.9)
    summed(30.0, 31.4, 38.0)
    for s in range(SWEEPS):
        sweep(s, 46.0 + 7 * s)
    finish(65.0)

    for _, _, f in sorted(events, key=lambda e: e[:2]):
        f()

    wait(tl.at[pl.ds(0, 7)], tsend)
    wait(icd.at[pl.ds(0, 7)], isend)
    for i in range(7):
        wait(codes.at[0], csend.at[i])
    for h in range(HALVES):
        for d in range(2):
            wait(hb.at[h, :, pl.ds(0, 3), :, pl.ds(0, 240), :], gsend.at[h, d])
    wait(sp, psend)
    wait(ts.at[pl.ds(0, 6)], ysend)
    for s in range(SWEEPS):
        wait(gat[s].at[pl.ds(0, 2)], ssend.at[s])
    wait(fin.at[pl.ds(0, 7)], fsend)
    wait(res, osem)


def per_device(kernels, history, incident, owner, pairs, tiles, counts):
    dma = pltpu.SemaphoreType.DMA
    any_ = pl.BlockSpec(memory_space=pl.ANY)
    return pl.pallas_call(
        body,
        out_shape=jax.ShapeDtypeStruct(incident.shape, F32),
        in_specs=[any_] * 7,
        out_specs=any_,
        scratch_shapes=[
            pltpu.VMEM((HALVES, 2, NX, LH, NZ * SRC, W), BF16),
            pltpu.VMEM((2 * NX, 8 * CL, DEPTH), BF16),
            pltpu.VMEM((HALVES, 8, CL, W), F32),
            *[pltpu.VMEM((8, W, CL), F32)] * 4,
            pltpu.VMEM((3, 8, CW, CL), F32),
            pltpu.VMEM((1, CL, COLS), F32),
            *[pltpu.VMEM((8, CW, CL), F32)] * 6,
            pltpu.VMEM((1, CL, COLS), F32),
            pltpu.VMEM((TILES, CL, CL), BF16),
            pltpu.VMEM((8, TILES, CL, CL), BF16),
            *[pltpu.VMEM((3, 8, CW, CL), BF16)] * SWEEPS,
            pltpu.SMEM((128,), jnp.int32),
            pltpu.SMEM((2, TILES), jnp.int32),
            pltpu.SMEM((1,), jnp.int32),
            pltpu.SMEM((8, 16), jnp.int32),
            dma((5,)), dma((8, LH)), dma((HALVES, 2)), dma((HALVES, 2, 5, 4)), dma((HALVES, 2)),
            dma((7,)), dma, dma((7,)), dma, dma((7,)), dma((7,)),
            dma((8,)), dma, dma((3, 2)), dma, dma((SWEEPS, 2, 2)), dma((SWEEPS,)), dma((7,)), dma, dma,
        ],
        compiler_params=pltpu.CompilerParams(
            collective_id=0, has_side_effects=True, vmem_limit_bytes=56 * 2**20
        ),
        cost_estimate=pl.CostEstimate(flops=5_200_000_000, bytes_accessed=21_000_000, transcendentals=0),
    )(kernels, history, incident, owner, pairs.T, tiles, counts)


def solution(mesh):
    both = ("row", "col")
    in_specs = (
        P(None, "col", "row"), P(None, both, None), P(both, None, None), P(),
        P(both, None), P(both, None, None), P(both),
    )
    return jax.shard_map(
        per_device, mesh=mesh, in_specs=in_specs, out_specs=P(both, None, None), check_vma=False
    )
```

```python
import functools

import jax
import jax.numpy as jnp
from jax import lax
from jax.experimental import pallas as pl
from jax.experimental.pallas import tpu as pltpu
from jax.sharding import PartitionSpec as P

MESH = pl.DeviceIdType.MESH
F32, BF16 = jnp.float32, jnp.bfloat16

SWEEPS = 3
DAMPING = 0.7

NX, NZ, NY = 4, 4, 4
LAGS, SRC, COLS, CL = 6, 96, 256, 128
HALVES = 2
W = COLS // HALVES
CW = COLS // 8
LH = LAGS // 2
DEPTH = LH * NZ * SRC
TILES = 12


def body(kernels, history, incident, owner, pairs, tiles, counts, out,
         hb, kb, acc, mine, sp, rp, ts, ry, inc, ict, icd, drv, den, fin, last, res, tin, tl,
         gat0, gat1, gat2, owner_s, pairs_s, counts_s, codes,
         lsem, ksem, hsem, gsem, gsend, tsem, tsend, isem, isend, csem, csend,
         psem, psend, ysem, ysend, ssem, ssend, fsem, fsend, osem):
    row, col = lax.axis_index("row"), lax.axis_index("col")
    y, core = lax.div(row, 2), lax.rem(row, 2)
    x, z = lax.div(col, NZ), lax.rem(col, NZ)
    other = 1 - core

    def at_col(dx, dz):
        return lax.rem(x + dx + NX, NX) * NZ + lax.rem(z + dz + NZ, NZ)

    def at_row(dy):
        return lax.rem(y + dy + NY, NY) * 2 + core

    def near_col(dc):
        return lax.rem(col + dc + NX * NZ, NX * NZ)

    def send(src, dst, ssem_, rsem_, r, c):
        pltpu.make_async_remote_copy(
            src_ref=src, dst_ref=dst, send_sem=ssem_, recv_sem=rsem_,
            device_id={"row": r, "col": c}, device_id_type=MESH,
        ).start()

    def wait(ref, sem):
        pltpu.make_async_copy(ref, ref, sem).wait()

    gat = (gat0, gat1, gat2)

    barrier = pltpu.get_barrier_semaphore()
    greet = [(row, at_col(1, 0)), (row, at_col(-1, 0)), (row, at_col(0, 1)), (row, at_col(0, -1))]
    greet += [(at_row(1), col), (at_row(-1), col), (at_row(2), col), (y * 2 + other, col)]
    greet += [(at_row(dy) + other - core, col) for dy in (1, 2, 3)]
    for r, c in greet:
        pl.semaphore_signal(barrier, inc=1, device_id={"row": r, "col": c}, device_id_type=MESH)

    def piece(h, a, dx, dz, lo=0, n=SRC):
        zr = pl.multiple_of(lax.rem(z + dz + NZ, NZ) * SRC + lo, 16)
        return hb.at[h, a, dx % NX, :, pl.ds(zr, n), :]

    def own(h, a):
        return history.at[pl.ds(a * LH, LH), :, pl.ds(h * W, W)]

    for h in range(HALVES):
        for a in range(2):
            pltpu.make_async_copy(own(h, a), piece(h, a, 0, 0), hsem.at[h, a]).start()
    pltpu.make_async_copy(owner, owner_s, lsem.at[0]).start()
    pltpu.make_async_copy(pairs, pairs_s, lsem.at[1]).start()
    pltpu.make_async_copy(counts, counts_s, lsem.at[2]).start()
    pl.semaphore_wait(barrier, len(greet))

    events = []

    def at(t):
        def add(f):
            events.append((t, len(events), f))
        return add

    def axis(a, phase):
        return ((1, 0), (0, 1))[(a + phase) % 2]

    def move(h, a, off, d, lo, n, sem, first=False):
        src = own(h, a) if first else piece(h, a, off[0], off[1], lo, n)
        zr = pl.multiple_of(lax.rem(z + off[1] + NZ, NZ) * SRC + lo, 16)
        dst = hb.at[h, a, (off[0] - d[0]) % NX, :, pl.ds(zr, n), :]
        send(src, dst, gsend.at[h, 0 if d[0] else 1], sem, row, at_col(d[0], d[1]))

    def neg(d):
        return (-d[0], -d[1])

    def mul(d, k):
        return (d[0] * k, d[1] * k)

    def add2(p, q):
        return (p[0] + q[0], p[1] + q[1])

    half = SRC // 2

    def spread(h, a, off, j, first=False):
        d = axis(a, 1)
        move(h, a, off, d, 0, SRC, gsem.at[h, a, j, 0], first)
        move(h, a, off, neg(d), 0, SRC, gsem.at[h, a, j, 1], first)

    def relay(h, a, off, j, d):
        lo, hi = add2(off, neg(d)), add2(off, d)
        wait(piece(h, a, *lo), gsem.at[h, a, j, 0])
        move(h, a, lo, d, 0, half, gsem.at[h, a, j, 2])
        wait(piece(h, a, *hi), gsem.at[h, a, j, 1])
        move(h, a, hi, neg(d), half, half, gsem.at[h, a, j, 3])

    def far(h, a, off, j, d):
        o = add2(off, mul(d, 2))
        wait(piece(h, a, o[0], o[1], 0, half), gsem.at[h, a, j, 2])
        wait(piece(h, a, o[0], o[1], half, half), gsem.at[h, a, j, 3])

    order = [(1, 0), (0, 0), (1, 3), (1, 1), (0, 3), (0, 1), (1, 2), (0, 2)]

    def mm(a, dx):
        g = a * NX + dx % NX
        for l in range(LH):
            wait(kb.at[g, :, pl.ds(l * NZ * SRC, NZ * SRC)], ksem.at[g, l])
        w = jnp.concatenate([hb[h, a, dx % NX].reshape(DEPTH, W) for h in range(HALVES)], axis=1)
        d = jnp.dot(kb[g], w, preferred_element_type=F32)
        for h in range(HALVES):
            part = d[:, h * W:(h + 1) * W].reshape(2 * NY, CL, W)
            acc[h] = part if (a, dx % NX) == order[0] else acc[h] + part

    def product(h, t0, a, dx):
        if h == HALVES - 1:
            @at(t0)
            def _():
                mm(a, dx)

    def gather(h, t0, u):
        @at(t0)
        def _():
            for a in range(2):
                d = axis(a, 0)
                move(h, a, (0, 0), d, 0, SRC, gsem.at[h, a, 0, 0], True)
                move(h, a, (0, 0), neg(d), 0, SRC, gsem.at[h, a, 0, 1], True)
            for a in range(2):
                spread(h, a, (0, 0), 1, True)

        @at(t0 + 1.2 * u)
        def _():
            for a in range(2):
                p = axis(a, 0)
                relay(h, a, (0, 0), 0, p)
            for a in range(2):
                p = axis(a, 0)
                spread(h, a, neg(p), 2)
                spread(h, a, p, 3)

        @at(t0 + 2.2 * u)
        def _():
            for a in range(2):
                relay(h, a, (0, 0), 1, axis(a, 1))

        @at(t0 + 2.7 * u)
        def _():
            for a in range(2):
                p = axis(a, 0)
                far(h, a, (0, 0), 0, p)
                spread(h, a, mul(p, 2), 4)
            for a in range(2):
                wait(piece(h, a, 0, 0), hsem.at[h, a])

        product(h, t0 + 2.7 * u, 1, 0)

        @at(t0 + 3.7 * u)
        def _():
            for a in range(2):
                relay(h, a, neg(axis(a, 0)), 2, axis(a, 1))

        @at(t0 + 4.7 * u)
        def _():
            for a in range(2):
                relay(h, a, axis(a, 0), 3, axis(a, 1))

        @at(t0 + 5.2 * u)
        def _():
            for a in range(2):
                far(h, a, (0, 0), 1, axis(a, 1))

        product(h, t0 + 5.2 * u, 0, 0)

        @at(t0 + 6.2 * u)
        def _():
            for a in range(2):
                relay(h, a, mul(axis(a, 0), 2), 4, axis(a, 1))

        product(h, t0 + 6.3 * u, 1, -1)

        product(h, t0 + 6.5 * u, 1, 1)

        @at(t0 + 6.8 * u)
        def _():
            for a in range(2):
                far(h, a, neg(axis(a, 0)), 2, axis(a, 1))

        product(h, t0 + 6.8 * u, 0, -1)

        @at(t0 + 7.3 * u)
        def _():
            for a in range(2):
                far(h, a, axis(a, 0), 3, axis(a, 1))

        product(h, t0 + 7.3 * u, 0, 1)

        @at(t0 + 7.8 * u)
        def _():
            far(h, 1, mul(axis(1, 0), 2), 4, axis(1, 1))

        product(h, t0 + 7.8 * u, 1, 2)

        @at(t0 + 7.8 * u)
        def _():
            far(h, 0, mul(axis(0, 0), 2), 4, axis(0, 1))

        product(h, t0 + 7.8 * u, 0, 2)

    part = core * NY + y
    peers = [(dy, flip) for dy in (2, 1, 3) for flip in (0, 1)] + [(0, 1)]

    def peer(dy, flip):
        y2 = lax.rem(y + dy, NY)
        k2 = other if flip else core
        return y2 * 2 + k2, k2 * NY + y2

    def position(r):
        p = jnp.int32(0)
        for b in range(NY * 2):
            p = p + jnp.where(owner_s[col * (NY * 2) + b] == r, b, 0)
        return jnp.minimum(p, NY * 2 - 1)

    tab = {}

    @at(1.0)
    def _():
        wait(tin, lsem.at[4])
        for t in range(TILES):
            tl[row, t] = tin[t].T
        for i, dy in enumerate((1, 3, 2)):
            send(tl.at[row], tl.at[row], tsend, tsem.at[i], peer(back(dy), 0)[0], col)
        send(tl.at[row], tl.at[row], tsend, tsem.at[3], y * 2 + other, col)

    @at(2.0)
    def _():
        wait(owner_s, lsem.at[0])
        wait(pairs_s, lsem.at[1])
        wait(counts_s, lsem.at[2])
        for t in range(TILES):
            s = jnp.clip(pairs_s[1, t], 0, CL - 1)
            zi = jnp.minimum(lax.rem(lax.shift_right_logical(s, 3) - col + 2 * NX * NZ + 1, NX * NZ), 2)
            codes[row, t] = jnp.where(t < counts_s[0], zi * (2 * NY) + owner_s[s], -1)
        for t in range(TILES, 16):
            codes[row, t] = -1
        wait(inc, lsem.at[3])
        for h in range(HALVES):
            ict[pl.ds(h * NY, NY)] = inc[0, :, h * W:(h + 1) * W].T.reshape(NY, CW, CL)
        icd[row] = ict[part]
        for i, (dy, flip) in enumerate(peers):
            r, p = peer(dy, flip)
            send(ict.at[p], icd.at[row], isend, isem.at[i], r, col)
            send(codes.at[row], codes.at[row], csend.at[i], csem.at[i], r, col)

    def exchange(t0):
        @at(t0)
        def _():
            for i, dy in enumerate((1, 3, 2)):
                r = peer(dy, 0)[0]
                wait(tl.at[r], tsem.at[i])
                send(tl.at[r], tl.at[r], tsend, tsem.at[4 + i], y * 2 + other, col)

    def back(dy):
        return (NY - dy) % NY

    def summed(t0, t1, t2):
        @at(t0)
        def _():
            pos = [position(jnp.int32(r)) for r in range(2 * NY)]
            for r in range(2 * NY):
                sp[r] = acc[other, pos[r]].T
                send(sp.at[r], rp.at[r], psend, psem.at[r], y * 2 + other, col)
            for r in range(2 * NY):
                mine[r] = acc[core, pos[r]].T

        @at(t1)
        def _():
            for g in range(NY):
                for r in range(g * 2, g * 2 + 2):
                    wait(rp.at[r], psem.at[r])
                    ts[r] = mine[r] + rp[r]
                for i, dy in enumerate((2, 1, 3)):
                    y2 = lax.rem(y + dy, NY)
                    send(ts.at[pl.ds(g * 2, 2), pl.ds(pl.multiple_of(y2 * CW, CW), CW)],
                         ry.at[i, pl.ds(g * 2, 2)], ysend, ysem.at[i, g], y2 * 2 + core, col)
            for i in range(7):
                dy, flip = peers[i]
                wait(icd.at[peer(back(dy), flip)[0]], isem.at[i])
            drv[...] = icd[...] - ts[:, pl.ds(pl.multiple_of(y * CW, CW), CW)]

        @at(t2)
        def _():
            for g in range(2):
                rows = pl.ds(g * NY, NY)
                for i in (1, 2, 0):
                    for q in (2 * g, 2 * g + 1):
                        wait(ry.at[i, pl.ds(q * 2, 2)], ysem.at[i, q])
                drv[rows] = drv[rows] - (ry[0, rows] + (ry[1, rows] + ry[2, rows]))
                gat[0][1, rows] = drv[rows].astype(BF16)
                halo(0, g)

    def halo(s, g):
        src = gat[s].at[1, pl.ds(g * NY, NY)]
        for i, (dc, zi) in enumerate(((1, 0), (-1, 2))):
            send(src, gat[s].at[zi, pl.ds(g * NY, NY)], ssend.at[s], ssem.at[s, i, g], row, near_col(dc))

    def sweep(s, t1):
        g = gat[s]

        def one(r):
            blocks = []
            for t in range(TILES):
                c = codes[r, t]
                i = jnp.clip(c, 0, 6 * NY - 1)
                u = g[lax.shift_right_logical(i, 3), lax.rem(i, 2 * NY)]
                blocks.append(jnp.where(c >= 0, u, jnp.zeros((), BF16)))
            near = jnp.dot(jnp.concatenate(blocks, axis=1), tl[r].reshape(TILES * CL, CL), preferred_element_type=F32)
            d = drv[r]
            cur = d if s == 0 else den[r]
            return cur + DAMPING * (d - cur - near)

        @at(t1)
        def _():
            if s == 0:
                for i, (dy, flip) in enumerate(peers):
                    wait(codes.at[peer(back(dy), flip)[0]], csem.at[i])
                for i, dy in enumerate((1, 3, 2)):
                    wait(tl.at[peer(dy, 1)[0]], tsem.at[4 + i])
                wait(tl.at[peer(0, 1)[0]], tsem.at[3])
            for k in range(2):
                for i, zi in enumerate((0, 2)):
                    wait(g.at[zi, pl.ds(k * NY, NY)], ssem.at[s, i, k])
            if s < SWEEPS - 1:
                for r in range(2 * NY):
                    new = one(r)
                    den[r] = new
                    gat[s + 1][1, r] = new.astype(BF16)
                    if r % NY == NY - 1:
                        halo(s + 1, r // NY)
            else:
                for i, (dy, flip) in enumerate(peers):
                    r = peer(dy, flip)[0]
                    fin[r] = one(r)
                    send(fin.at[r], last.at[part], fsend, fsem.at[i], r, col)
                last[part] = one(row)

    def finish(t0):
        @at(t0)
        def _():
            for i, (dy, flip) in enumerate(peers):
                wait(last.at[peer(back(dy), flip)[1]], fsem.at[i])
            for h in range(HALVES):
                res[0, :, h * W:(h + 1) * W] = last[pl.ds(h * NY, NY)].reshape(W, CL).T
            pltpu.make_async_copy(res, out, osem).start()

    def loads():
        pltpu.make_async_copy(incident, inc, lsem.at[3]).start()
        pltpu.make_async_copy(tiles, tin, lsem.at[4]).start()
        for a, rel in order:
            gx = lax.rem(x + rel, NX)
            for l in range(LH):
                pltpu.make_async_copy(
                    kernels.at[a * LH + l, :, pl.ds(pl.multiple_of(gx * (NZ * SRC), 128), NZ * SRC)],
                    kb.at[a * NX + rel, :, pl.ds(l * NZ * SRC, NZ * SRC)],
                    ksem.at[a * NX + rel, l],
                ).start()

    events.append((0.02, 1000, loads))

    gather(0, 0.0, 3.2)
    gather(1, 0.01, 3.2)
    exchange(24.9)
    summed(30.0, 31.4, 38.0)
    for s in range(SWEEPS):
        sweep(s, 46.0 + 7 * s)
    finish(65.0)

    for _, _, f in sorted(events, key=lambda e: e[:2]):
        f()

    wait(tl.at[pl.ds(0, 7)], tsend)
    wait(icd.at[pl.ds(0, 7)], isend)
    for i in range(7):
        wait(codes.at[0], csend.at[i])
    for h in range(HALVES):
        for d in range(2):
            wait(hb.at[h, :, pl.ds(0, 3), :, pl.ds(0, 240), :], gsend.at[h, d])
    wait(sp, psend)
    wait(ts.at[pl.ds(0, 6)], ysend)
    for s in range(SWEEPS):
        wait(gat[s].at[pl.ds(0, 2)], ssend.at[s])
    wait(fin.at[pl.ds(0, 7)], fsend)
    wait(res, osem)


def per_device(kernels, history, incident, owner, pairs, tiles, counts):
    dma = pltpu.SemaphoreType.DMA
    any_ = pl.BlockSpec(memory_space=pl.ANY)
    return pl.pallas_call(
        body,
        out_shape=jax.ShapeDtypeStruct(incident.shape, F32),
        in_specs=[any_] * 7,
        out_specs=any_,
        scratch_shapes=[
            pltpu.VMEM((HALVES, 2, NX, LH, NZ * SRC, W), BF16),
            pltpu.VMEM((2 * NX, 8 * CL, DEPTH), BF16),
            pltpu.VMEM((HALVES, 8, CL, W), F32),
            *[pltpu.VMEM((8, W, CL), F32)] * 4,
            pltpu.VMEM((3, 8, CW, CL), F32),
            pltpu.VMEM((1, CL, COLS), F32),
            *[pltpu.VMEM((8, CW, CL), F32)] * 6,
            pltpu.VMEM((1, CL, COLS), F32),
            pltpu.VMEM((TILES, CL, CL), BF16),
            pltpu.VMEM((8, TILES, CL, CL), BF16),
            *[pltpu.VMEM((3, 8, CW, CL), BF16)] * SWEEPS,
            pltpu.SMEM((128,), jnp.int32),
            pltpu.SMEM((2, TILES), jnp.int32),
            pltpu.SMEM((1,), jnp.int32),
            pltpu.SMEM((8, 16), jnp.int32),
            dma((5,)), dma((8, LH)), dma((HALVES, 2)), dma((HALVES, 2, 5, 4)), dma((HALVES, 2)),
            dma((7,)), dma, dma((7,)), dma, dma((7,)), dma((7,)),
            dma((8,)), dma, dma((3, NY)), dma, dma((SWEEPS, 2, 2)), dma((SWEEPS,)), dma((7,)), dma, dma,
        ],
        compiler_params=pltpu.CompilerParams(
            collective_id=0, has_side_effects=True, vmem_limit_bytes=56 * 2**20
        ),
        cost_estimate=pl.CostEstimate(flops=5_200_000_000, bytes_accessed=21_000_000, transcendentals=0),
    )(kernels, history, incident, owner, pairs.T, tiles, counts)


def solution(mesh):
    both = ("row", "col")
    in_specs = (
        P(None, "col", "row"), P(None, both, None), P(both, None, None), P(),
        P(both, None), P(both, None, None), P(both),
    )
    return jax.shard_map(
        per_device, mesh=mesh, in_specs=in_specs, out_specs=P(both, None, None), check_vma=False
    )
```
